128 devices in a mesh: pair: 8 (over x, z_lo), row: 4 (over z_hi, core), col: 4 (over y).
Axes of the slice: x: 4, y: 4, z: 4 (z_hi: 2, z_lo: 2; z = z_hi * 2 + z_lo), core: 2. Of those that a mesh axis runs over, the one named last changes fastest.
Arguments:
- valence_index: int32 [4096], P(('pair', 'row', 'col')), may hold values from 0 to 63, as said below
- conduction_index: int32 [4096], P(('pair', 'row', 'col')), may hold values from 0 to 63
- valence_waves: bfloat16 [64, 2, 32768], replicated, may hold values from -6 to 6
- conduction_waves: bfloat16 [64, 2, 32768], replicated, may hold values from -6 to 6
- valence_energy: float32 [64], replicated, may hold values from -1 to -0.05
- conduction_energy: float32 [64], replicated, may hold values from 0.05 to 1
- frequency: float32 [1], replicated, may hold values from 0.2 to 1
- sphere_map: int32 [8192], replicated, may hold values from 0 to 32767, as said below
Outputs:
- chi_zero: float32 [8192, 2, 8192], P(('pair', 'row'), None, 'col')
The draws below stay inside these ranges and needn't reach their ends.
Inputs may be any that keep to these rules, and one draw needn't show every extreme that they name: The pairs (valence_index[p], conduction_index[p]) are all different. `sphere_map`: all entries are different.
All inputs are finite; a program needn't handle non-finite values.
Results may differ from the reference program's by a relative error of at most 0.011.
Values may be sent and summed in bfloat16 or wider, within the bound.
No kernel may reach another device: no remote copies, remote signals or barrier semaphores. Data moves between devices by JAX's collectives and lax.ppermute only.
A program may use at most 192 MiB of HBM per device.

```python
import math
import jax
import jax.numpy as jnp
from jax import lax

GRID = 32
G = 8192
VB = 64
CB = 64
PAIRS = 4096


def shared_pairs(key):
    return jax.random.permutation(key, VB * CB)[:PAIRS].astype(jnp.int32)


def draw_valence_index(key, part):
    return shared_pairs(key) // CB


def draw_conduction_index(key, part):
    return shared_pairs(key) % CB


def draw_sphere_map(key, part):
    key = jax.random.fold_in(key, 7)
    first_key, second_key = jax.random.split(key)
    chosen = jax.random.permutation(first_key, GRID ** 3 - 1)[:G - 1].astype(jnp.int32)
    chosen = jnp.concatenate([chosen, jnp.array([GRID ** 3 - 1], jnp.int32)])
    order = jax.random.permutation(second_key, G)
    return chosen[order].astype(jnp.int32)


def scatter_about(own_key, dims, scale, reach, held_as=jnp.bfloat16):
    entries = scale * jax.random.normal(own_key, dims, jnp.float32)
    return jnp.clip(entries, min=-reach, max=reach).astype(held_as)


def setup_inputs(seed: int = 0) -> dict:
    seeds = jax.random.split(jax.random.key(seed), 9)
    return {
        "valence_index": draw_valence_index(jax.random.fold_in(seeds[8], 71), 0),
        "conduction_index": draw_conduction_index(jax.random.fold_in(seeds[8], 71), 0),
        "valence_waves": scatter_about(seeds[2], (VB, 2, GRID ** 3), 1.0, 6.0),
        "conduction_waves": scatter_about(seeds[3], (CB, 2, GRID ** 3), 1.0, 6.0),
        "valence_energy": jnp.clip(jax.random.uniform(seeds[4], (VB,), jnp.float32, -1.0, -0.05), -1.0, -0.05),
        "conduction_energy": jnp.clip(jax.random.uniform(seeds[5], (CB,), jnp.float32, 0.05, 1.0), 0.05, 1.0),
        "frequency": jnp.clip(jax.random.uniform(seeds[6], (1,), jnp.float32, 0.2, 1.0), 0.2, 1.0),
        "sphere_map": draw_sphere_map(jax.random.fold_in(seeds[8], 71), 0),
    }


def block_densities(indices, valence_waves, conduction_waves, sphere_map):
    valence = valence_waves[indices[0]].astype(jnp.float32)
    conduction = conduction_waves[indices[1]].astype(jnp.float32)
    real_part = valence[:, 0] * conduction[:, 0] + valence[:, 1] * conduction[:, 1]
    imag_part = valence[:, 0] * conduction[:, 1] - valence[:, 1] * conduction[:, 0]
    pairs_here = real_part.shape[0]
    field = (real_part + 1j * imag_part).reshape(pairs_here, GRID, GRID, GRID)
    spectrum = jnp.fft.fftn(field, axes=(1, 2, 3)).reshape(pairs_here, GRID ** 3)
    spectrum = spectrum / math.sqrt(GRID ** 3)
    picked = spectrum[:, sphere_map]
    return jnp.stack([jnp.real(picked), jnp.imag(picked)], 1).astype(jnp.bfloat16)

def reference(valence_index, conduction_index, valence_waves, conduction_waves, valence_energy, conduction_energy, frequency, sphere_map):
    block_size = math.gcd(PAIRS, 128)
    grouped = jnp.stack([valence_index.reshape(-1, block_size), conduction_index.reshape(-1, block_size)], 1)
    rho = lax.map(lambda indices: block_densities(indices, valence_waves, conduction_waves, sphere_map), grouped)
    rho = rho.reshape(PAIRS, 2, G)
    gap = conduction_energy[conduction_index] - valence_energy[valence_index]
    weight = 4.0 * gap / (gap * gap + frequency[0] * frequency[0]) / PAIRS
    weighted = (weight[:, None, None] * rho.astype(jnp.float32)).astype(jnp.bfloat16)
    right_side = jnp.concatenate([rho[:, 0], rho[:, 1]], 0).astype(jnp.float32)
    left_real = jnp.concatenate([weighted[:, 0], weighted[:, 1]], 0).astype(jnp.float32)
    left_imag = jnp.concatenate([weighted[:, 1], -weighted[:, 0]], 0).astype(jnp.float32)
    chi_real = jnp.dot(left_real.T, right_side, preferred_element_type=jnp.float32)
    chi_imag = jnp.dot(left_imag.T, right_side, preferred_element_type=jnp.float32)
    return jnp.stack([chi_real, chi_imag], 1)
```

```python
import numpy as np
import jax, jax.numpy as jnp
from jax import lax
from jax.experimental import pallas as pl
from jax.sharding import Mesh, PartitionSpec as P
from jax.experimental.pallas import tpu as pltpu


def tables():
    x = np.arange(32); e = np.arange(8); b = np.arange(4)
    ka, kx = np.meshgrid(e, x, indexing="ij")
    xx, yh = np.meshgrid(x, e, indexing="ij")
    ph = (kx.reshape(-1,1)*xx.reshape(1,-1) + 4*ka.reshape(-1,1)*yh.reshape(1,-1)) % 32
    c, s = np.cos(2*np.pi*ph/32), np.sin(2*np.pi*ph/32)
    first = np.block([[c, s], [-s, c]])
    second = []
    kb, kz = np.meshgrid(b, x, indexing="ij")
    yl, z = np.meshgrid(b, x, indexing="ij")
    for a in range(8):
        ky = a + 8*kb.reshape(-1,1)
        ph = (kz.reshape(-1,1)*z.reshape(1,-1) + ky*yl.reshape(1,-1)) % 32
        second.append(np.concatenate([np.cos(2*np.pi*ph/32), np.sin(2*np.pi*ph/32)], 1))
    return first.astype(jnp.bfloat16), np.stack(second).astype(jnp.bfloat16)

def density_kernel(pos, place, val, con, first, second, scale, *rest):
    outs, (xs, yr, yi, zt, held) = rest[:8], rest[8:]
    v = pl.program_id(0)
    vr = val[v, 0].astype(jnp.float32)
    vi = val[v, 1].astype(jnp.float32)
    for pair in range(4):
        for k in range(2):
            cr = con[2*pair+k, 0].astype(jnp.float32)
            ci = con[2*pair+k, 1].astype(jnp.float32)
            xs[0:256, k*128:(k+1)*128] = (vr*cr + vi*ci).astype(jnp.bfloat16)
            xs[256:512, k*128:(k+1)*128] = (vr*ci - vi*cr).astype(jnp.bfloat16)
        y = jnp.dot(first[...], xs[...], preferred_element_type=jnp.float32)
        for k in range(2):
            p = v*8 + 2*pair + k
            yr[pl.ds(p, 256, stride=64), :] = y[0:256, k*128:(k+1)*128]
            yi[pl.ds(p, 256, stride=64), :] = y[256:512, k*128:(k+1)*128]

    @pl.when(v == 7)
    def _():
        def side(r):
            ar = yr[pl.ds(pl.multiple_of(r*64, 64), 64), :].astype(jnp.bfloat16)
            ai = yi[pl.ds(pl.multiple_of(r*64, 64), 64), :].astype(jnp.bfloat16)
            return [jnp.concatenate([ar, ai], 1), jnp.concatenate([ai, -ar], 1)]
        @pl.loop(0, 128, unroll=4)
        def _(q):
            r = q*2
            right = jnp.concatenate(side(r) + side(r+1), 0)
            z = lax.dot_general(second[r // 32], right, (((1,), (1,)), ((), ())), preferred_element_type=jnp.float32)
            zt[pl.ds(pl.multiple_of(r*128, 128), 128), :] = z[:, 0:128]
            zt[pl.ds(pl.multiple_of(r*128+128, 128), 128), :] = z[:, 128:256]
        w = scale[...]
        @pl.loop(0, 256, unroll=2)
        def _(q):
            rows = [zt[pl.ds(pos[q*16+j], 1), :] for j in range(16)]
            t = jnp.concatenate(rows, 0) * w
            held[pl.ds(pl.multiple_of(q*16, 16), 16), :] = t.astype(jnp.bfloat16)
        for s in range(4):
            a = pl.multiple_of(lax.rem(place[0]+s, 4)*1024, 1024)
            outs[s][...] = held[pl.ds(a, 1024), :]
            b = pl.multiple_of(lax.rem(place[1]+s, 4)*1024, 1024)
            outs[4+s][...] = held[pl.ds(b, 1024), :]

def densities(pos, place, val, con, scale):
    first, second = tables()
    full = lambda shape: pl.BlockSpec(shape, lambda i, *_: (0,)*len(shape))
    return pl.pallas_call(
        density_kernel,
        grid_spec=pltpu.PrefetchScalarGridSpec(
            num_scalar_prefetch=2, grid=(8,),
            in_specs=[full((8,2,256,128)), full((8,2,256,128)), full((512,512)), full((8,128,256)), full((1,128))],
            out_specs=[full((1024,128))]*8,
            scratch_shapes=[pltpu.VMEM((512,256), jnp.bfloat16), pltpu.VMEM((16384,128), jnp.float32),
                pltpu.VMEM((16384,128), jnp.float32), pltpu.VMEM((32768,128), jnp.float32), pltpu.VMEM((4096,128), jnp.bfloat16)],
        ),
        out_shape=[jax.ShapeDtypeStruct((1024,128), jnp.bfloat16)]*8,
        compiler_params=pltpu.CompilerParams(vmem_limit_bytes=56*2**20),
        name="densities",
    )(pos, place, val, con, jnp.asarray(first), jnp.asarray(second), scale)


def product_kernel(core, *refs):
    rows, own, other = refs[0:4], refs[4:8], refs[8:12]
    out, left, right = refs[12:]
    step = pl.program_id(0)

    @pl.when(step == 0)
    def _():
        for t in range(4):
            for s in range(4):
                k = (t*4 + s)*128
                left[:, k:k+128] = rows[t][s]

    lane = lax.broadcasted_iota(jnp.int32, (1, 128), 1)
    sign = jnp.where(lane < 64, -1.0, 1.0)

    def fill(cols):
        for t in range(4):
            for s in range(4):
                k = (t*4 + s)*128
                piece = cols[s][t]
                right[0:256, k:k+128] = piece
                turned = pltpu.roll(piece.astype(jnp.float32), 64, 1) * sign
                right[256:512, k:k+128] = turned.astype(jnp.bfloat16)

    half = lax.rem(step, 2)

    @pl.when(half == 0)
    def _():
        fill(own)

    @pl.when(half == 1)
    def _():
        fill(other)

    tile = lax.dot_general(left[...], right[...], (((1,), (1,)), ((), ())), preferred_element_type=jnp.float32)
    tile = tile.astype(jnp.bfloat16)
    for j in range(4):
        place = (j % 2)*2 + j//2
        for o in range(2):
            out[place, o] = tile[j*256:(j+1)*256, o*256:(o+1)*256]


def product(core, rows, own, other, first, count):
    full = pl.BlockSpec((4, 1024, 128), lambda n, core: (0, 0, 0))
    part = pl.BlockSpec((4, 256, 128), lambda n, core: (0, first + n//2, 0))
    return pl.pallas_call(
        product_kernel,
        grid_spec=pltpu.PrefetchScalarGridSpec(
            num_scalar_prefetch=1, grid=(2*count,),
            in_specs=[full]*4 + [part]*8,
            out_specs=pl.BlockSpec(
                (4, 2, 256, 256),
                lambda n, core: (0, 0, 0, 2*(n//2) + core[0] + n % 2 - 2*core[0]*(n % 2))),
            scratch_shapes=[pltpu.VMEM((1024, 2048), jnp.bfloat16), pltpu.VMEM((512, 2048), jnp.bfloat16)],
        ),
        out_shape=jax.ShapeDtypeStruct((4, 2, 256, 512*count), jnp.bfloat16),
        compiler_params=pltpu.CompilerParams(vmem_limit_bytes=48*2**20),
        cost_estimate=pl.CostEstimate(flops=2*1024*512*2048*2*count, bytes_accessed=16*2**20, transcendentals=0),
        name="product",
    )(core, *rows, *own, *other)


def ring(shift):
    return [(i, (i + shift) % 4) for i in range(4)]


CHUNKS = 4


def local(valence_index, conduction_index, valence_waves, conduction_waves,
          valence_energy, conduction_energy, frequency, sphere_map):
    x, y = lax.axis_index("x"), lax.axis_index("y")
    zl, zh, core = lax.axis_index("zl"), lax.axis_index("zh"), lax.axis_index("core")
    vb, cb = (y*2 + zl)*8, (x*2 + zh)*8
    val = lax.dynamic_slice(valence_waves, (vb, 0, 0), (8, 2, 32768)).reshape(8, 2, 256, 128)
    con = lax.dynamic_slice(conduction_waves, (cb, 0, 0), (8, 2, 32768)).reshape(8, 2, 256, 128)
    gap = lax.dynamic_slice(conduction_energy, (cb,), (8,))[None, :] - lax.dynamic_slice(valence_energy, (vb,), (8,))[:, None]
    weight = 4.0 * gap / (gap*gap + frequency[0]*frequency[0]) / 4096
    scale = jnp.sqrt(weight / 32768.0).reshape(1, 64)
    scale = jnp.concatenate([scale, scale], 1)
    point = lax.dynamic_index_in_dim(sphere_map.reshape(16, 2, 256), core, 1, keepdims=False).reshape(4096)
    ky = (point >> 5) & 31
    pos = ((ky & 7)*32 + (point >> 10))*128 + (ky >> 3)*32 + (point & 31)
    parts = densities(pos, jnp.stack([x, y]).astype(jnp.int32), val, con, scale)
    row = [parts[0]] + [None]*3
    col = [parts[4]] + [None]*3
    for s in (2, 1, 3):
        row[s] = lax.ppermute(parts[s], "x", ring(s))
        col[s] = lax.ppermute(parts[4 + s], "y", ring(s))
    rows = [jnp.stack(row)] + [None]*3
    own = [jnp.stack(col)] + [None]*3
    for s in (1, 3, 2):
        rows[s] = lax.ppermute(rows[0], "y", ring(s))
        own[s] = lax.ppermute(own[0], "x", ring(s))
    other = [lax.ppermute(a, "core", [(0, 1), (1, 0)]) for a in own]
    which = core.astype(jnp.int32)[None]
    done = []
    for q in range(CHUNKS):
        count = 4 // CHUNKS
        tile = product(which, rows, own, other, q*count, count)
        tile = tile.reshape(4, 512, 512*count)
        total = lax.psum_scatter(tile, ("zh", "zl"), scatter_dimension=0, tiled=True)
        done.append(total.reshape(2, 256, 512*count))
    whole = jnp.concatenate(done, 2)
    return jnp.transpose(whole, (1, 0, 2)).astype(jnp.float32)


def solution(mesh):
    shaped = Mesh(mesh.devices.reshape(4, 2, 2, 2, 4), ("x", "zl", "zh", "core", "y"))
    split = P(("x", "zl", "zh", "core", "y"))
    return jax.shard_map(
        local,
        mesh=shaped,
        in_specs=(split, split, P(), P(), P(), P(), P(), P()),
        out_specs=P(("x", "zl", "zh", "core"), None, "y"),
        check_vma=False,
    )
```

```python
import numpy as np
import jax, jax.numpy as jnp
from jax import lax
from jax.experimental import pallas as pl
from jax.sharding import Mesh, PartitionSpec as P
from jax.experimental.pallas import tpu as pltpu

VMEM = 60*2**20


def tables():
    x = np.arange(32); e = np.arange(8); b = np.arange(4)
    ka, kx = np.meshgrid(e, x, indexing="ij")
    xx, yh = np.meshgrid(x, e, indexing="ij")
    ph = (kx.reshape(-1,1)*xx.reshape(1,-1) + 4*ka.reshape(-1,1)*yh.reshape(1,-1)) % 32
    c, s = np.cos(2*np.pi*ph/32), np.sin(2*np.pi*ph/32)
    first = np.block([[c, s], [-s, c]])
    second = []
    kb, kz = np.meshgrid(b, x, indexing="ij")
    yl, z = np.meshgrid(b, x, indexing="ij")
    for a in range(8):
        ky = a + 8*kb.reshape(-1,1)
        ph = (kz.reshape(-1,1)*z.reshape(1,-1) + ky*yl.reshape(1,-1)) % 32
        second.append(np.concatenate([np.cos(2*np.pi*ph/32), np.sin(2*np.pi*ph/32)], 1))
    return first.astype(jnp.bfloat16), np.stack(second).astype(jnp.bfloat16)

def density_kernel(pos, place, val, con, first, second, scale, *rest):
    outs, (xs, yr, yi, zt, held) = rest[:8], rest[8:]
    v = pl.program_id(0)
    vr = val[v, 0].astype(jnp.float32)
    vi = val[v, 1].astype(jnp.float32)
    for pair in range(4):
        for k in range(2):
            cr = con[2*pair+k, 0].astype(jnp.float32)
            ci = con[2*pair+k, 1].astype(jnp.float32)
            xs[0:256, k*128:(k+1)*128] = (vr*cr + vi*ci).astype(jnp.bfloat16)
            xs[256:512, k*128:(k+1)*128] = (vr*ci - vi*cr).astype(jnp.bfloat16)
        y = jnp.dot(first[...], xs[...], preferred_element_type=jnp.float32)
        for k in range(2):
            p = v*8 + 2*pair + k
            yr[pl.ds(p, 256, stride=72), :] = y[0:256, k*128:(k+1)*128]
            yi[pl.ds(p, 256, stride=72), :] = y[256:512, k*128:(k+1)*128]

    @pl.when(v == 7)
    def _():
        def side(r):
            ar = yr[pl.ds(pl.multiple_of(r*72, 8), 64), :].astype(jnp.bfloat16)
            ai = yi[pl.ds(pl.multiple_of(r*72, 8), 64), :].astype(jnp.bfloat16)
            return [jnp.concatenate([ar, ai], 1), jnp.concatenate([ai, -ar], 1)]
        @pl.loop(0, 128, unroll=8)
        def _(q):
            r = q*2
            right = jnp.concatenate(side(r) + side(r+1), 0)
            z = lax.dot_general(second[r // 32], right, (((1,), (1,)), ((), ())), preferred_element_type=jnp.float32)
            zt[pl.ds(pl.multiple_of(r*128, 128), 128), :] = z[:, 0:128]
            zt[pl.ds(pl.multiple_of(r*128+128, 128), 128), :] = z[:, 128:256]
        w = scale[...]
        @pl.loop(0, 256, unroll=2)
        def _(q):
            rows = [zt[pl.ds(pos[q*16+j], 1), :] for j in range(16)]
            t = jnp.concatenate(rows, 0) * w
            held[pl.ds(pl.multiple_of(q*16, 16), 16), :] = t.astype(jnp.bfloat16)
        for s in range(4):
            a = lax.rem(place[0]+s, 4)*1024
            for q, shift in enumerate((2, 1, 3, 0)):
                to = lax.rem(place[2]+shift, 4)
                block = lax.rem(to, 2)*2 + lax.div(to, 2)
                outs[s][q*256:(q+1)*256, :] = held[pl.ds(pl.multiple_of(a + block*256, 256), 256), :]
            b = lax.rem(place[1]+s, 4)*1024
            for q in range(4):
                outs[4+s][:, q*256:(q+1)*256] = held[pl.ds(pl.multiple_of(b + q*256, 256), 256), :].T


def densities(pos, place, val, con, scale):
    first, second = tables()
    full = lambda shape: pl.BlockSpec(shape, lambda i, *_: (0,)*len(shape))
    return pl.pallas_call(
        density_kernel,
        grid_spec=pltpu.PrefetchScalarGridSpec(
            num_scalar_prefetch=2, grid=(8,),
            in_specs=[full((8,2,256,128)), full((8,2,256,128)), full((512,512)), full((8,128,256)), full((1,128))],
            out_specs=[full((1024,128))]*4 + [full((128,1024))]*4,
            scratch_shapes=[pltpu.VMEM((512,256), jnp.bfloat16), pltpu.VMEM((256*72,128), jnp.float32),
                pltpu.VMEM((256*72,128), jnp.float32), pltpu.VMEM((32768,128), jnp.float32), pltpu.VMEM((4096,128), jnp.bfloat16)],
        ),
        out_shape=[jax.ShapeDtypeStruct((1024,128), jnp.bfloat16)]*4 + [jax.ShapeDtypeStruct((128,1024), jnp.bfloat16)]*4,
        compiler_params=pltpu.CompilerParams(vmem_limit_bytes=VMEM),
        name="densities",
    )(pos, place, val, con, jnp.asarray(first), jnp.asarray(second), scale)


def product_kernel(core, *refs):
    rows, own, other = refs[0:4], refs[4:8], refs[8:12]
    outs, (left, right) = refs[12:16], refs[16:]
    step = pl.program_id(0)

    @pl.when(step == 0)
    def _():
        for t in range(4):
            for s in range(4):
                k = (t*4 + s)*128
                left[:, k:k+128] = rows[t][s]

    def fill(cols):
        for t in range(4):
            for s in range(4):
                k = (t*4 + s)*128
                piece = cols[s][t]
                right[k:k+128, 0:256] = piece
                right[k:k+64, 256:512] = -piece[64:128]
                right[k+64:k+128, 256:512] = piece[0:64]

    @pl.when(step < 2)
    def _():
        fill(own)

    @pl.when(step >= 2)
    def _():
        fill(other)

    tile = jnp.dot(left[...], right[...], preferred_element_type=jnp.float32)
    tile = tile.astype(jnp.bfloat16)
    for h in range(2):
        @pl.when(lax.rem(step, 2) == h)
        def _(h=h):
            for b in range(2):
                for o in range(2):
                    outs[2*b + h][o] = tile[b*256:(b+1)*256, o*256:(o+1)*256]


def product(core, rows, own, other):
    full = pl.BlockSpec((4, 512, 128), lambda n, core: (0, 0, 0))
    near = pl.BlockSpec((4, 128, 256), lambda n, core: (0, 0, jnp.minimum(n, 1)))
    far = pl.BlockSpec((4, 128, 256), lambda n, core: (0, 0, jnp.maximum(n - 2, 0)))
    out = pl.BlockSpec(
        (2, 256, 256),
        lambda n, core: (0, 0, core[0] + n//2 - 2*core[0]*(n//2)))
    return pl.pallas_call(
        product_kernel,
        grid_spec=pltpu.PrefetchScalarGridSpec(
            num_scalar_prefetch=1, grid=(4,),
            in_specs=[full]*4 + [near]*4 + [far]*4,
            out_specs=[out]*4,
            scratch_shapes=[pltpu.VMEM((512, 2048), jnp.bfloat16), pltpu.VMEM((2048, 512), jnp.bfloat16)],
        ),
        out_shape=[jax.ShapeDtypeStruct((2, 256, 512), jnp.bfloat16)]*4,
        compiler_params=pltpu.CompilerParams(vmem_limit_bytes=VMEM),
        cost_estimate=pl.CostEstimate(flops=2**10, bytes_accessed=2**10, transcendentals=0),
        name="product",
    )(core, *rows, *own, *other)


def total_kernel(*refs):
    out = refs[-1]
    for h in range(2):
        t = refs[3*h][...].astype(jnp.float32) + refs[3*h+1][...].astype(jnp.float32)
        t = t + refs[3*h+2][...].astype(jnp.float32)
        out[:, 0, h*512:(h+1)*512] = t[0]
        out[:, 1, h*512:(h+1)*512] = t[1]


def total(parts, chunk, before):
    spec = pl.BlockSpec((2, 64, 512), lambda n: (0, n, 0))
    more = [] if before is None else [before]
    return pl.pallas_call(
        total_kernel,
        grid=(4,),
        in_specs=[spec]*6 + [pl.BlockSpec(memory_space=pl.ANY)]*len(more),
        out_specs=pl.BlockSpec((64, 2, 1024), lambda n: (n, 0, chunk)),
        out_shape=jax.ShapeDtypeStruct((256, 2, 2048), jnp.float32),
        input_output_aliases={6: 0} if more else {},
        compiler_params=pltpu.CompilerParams(vmem_limit_bytes=VMEM),
        cost_estimate=pl.CostEstimate(flops=2**10, bytes_accessed=2**10, transcendentals=0),
        name="total",
    )(*parts, *more)


def ring(shift):
    return [(i, (i + shift) % 4) for i in range(4)]


def along_z(block, shift):
    place = lambda z: (z % 2)*2 + z//2
    return lax.ppermute(block, ("zl", "zh"), [(place(i), place((i + shift) % 4)) for i in range(4)])


def after(arrays, *first):
    return lax.optimization_barrier((tuple(arrays), first))[0]


def spread(row, col, *first):
    rows, cols = [row] + [None]*3, [col] + [None]*3
    for s in (1, 3):
        rows[s] = lax.ppermute(row, "y", ring(s))
        cols[s] = lax.ppermute(col, "x", ring(s))
    row, col = after((row, col), rows[1], cols[1], rows[3], cols[3], *first)
    rows[2] = lax.ppermute(row, "y", ring(2))
    cols[2] = lax.ppermute(col, "x", ring(2))
    return rows, cols


def add(a, b):
    return (a.astype(jnp.float32) + b.astype(jnp.float32)).astype(jnp.bfloat16)


def begun(far):
    far0, far1, next0, next1 = far
    return next0, along_z(far0, 1), along_z(far1, -1), along_z(next1, 1)


def ended(far, near):
    next0, got0, got1, up1 = far
    last0, last1, mine0, mine1 = near
    down0 = along_z(last0, -1)
    up0, down1 = along_z(add(next0, got0), 1), along_z(add(last1, got1), -1)
    return [mine0, up0, down0, mine1, up1, down1]


def swapped(blocks):
    return [lax.ppermute(a, "core", [(0, 1), (1, 0)]) for a in blocks]


def local(valence_index, conduction_index, valence_waves, conduction_waves,
          valence_energy, conduction_energy, frequency, sphere_map):
    x, y = lax.axis_index("x"), lax.axis_index("y")
    zl, zh, core = lax.axis_index("zl"), lax.axis_index("zh"), lax.axis_index("core")
    vb, cb = (y*2 + zl)*8, (x*2 + zh)*8
    val = lax.dynamic_slice(valence_waves, (vb, 0, 0), (8, 2, 32768)).reshape(8, 2, 256, 128)
    con = lax.dynamic_slice(conduction_waves, (cb, 0, 0), (8, 2, 32768)).reshape(8, 2, 256, 128)
    gap = lax.dynamic_slice(conduction_energy, (cb,), (8,))[None, :] - lax.dynamic_slice(valence_energy, (vb,), (8,))[:, None]
    weight = 4.0 * gap / (gap*gap + frequency[0]*frequency[0]) / 4096
    scale = jnp.sqrt(weight / 32768.0).reshape(1, 64)
    scale = jnp.concatenate([scale, scale], 1)
    point = lax.dynamic_index_in_dim(sphere_map.reshape(16, 2, 256), core, 1, keepdims=False).reshape(4096)
    ky = (point >> 5) & 31
    pos = ((ky & 7)*32 + (point >> 10))*128 + (ky >> 3)*32 + (point & 31)
    place = jnp.stack([x, y, zh*2 + zl]).astype(jnp.int32)
    parts = densities(pos, place, val, con, scale)
    row = [parts[0]] + [None]*3
    col = [parts[4]] + [None]*3
    for s in (2, 1, 3):
        row[s] = lax.ppermute(parts[s], "x", ring(s))
        col[s] = lax.ppermute(parts[4 + s], "y", ring(s))
    row, col = jnp.stack(row), jnp.stack(col)
    which = core.astype(jnp.int32)[None]
    row_a, col_a = row[:, :512], col[:, :, :512]
    row_b, col_b = row[:, 512:], col[:, :, 512:]
    rows_a, own_a = spread(row_a, col_a)
    other_a = swapped(own_a)
    row_b, col_b = after((row_b, col_b), rows_a[2], own_a[2])
    aa = begun(product(which, rows_a, own_a, other_a))
    rows_b, own_b = spread(row_b, col_b, aa[0])
    other_b = swapped(after(own_b, aa[1], aa[2]))
    ba = product(which, rows_b, own_a, other_a)
    ab = begun(product(which, rows_a, own_b, other_b))
    bb = product(which, rows_b, own_b, other_b)
    return total(ended(ab, bb), 1, total(ended(aa, ba), 0, None))


def solution(mesh):
    shaped = Mesh(mesh.devices.reshape(4, 2, 2, 2, 4), ("x", "zl", "zh", "core", "y"))
    split = P(("x", "zl", "zh", "core", "y"))
    return jax.shard_map(
        local,
        mesh=shaped,
        in_specs=(split, split, P(), P(), P(), P(), P(), P()),
        out_specs=P(("x", "zl", "zh", "core"), None, "y"),
        check_vma=False,
    )
```

```python
import numpy as np
import jax, jax.numpy as jnp
from jax import lax
from jax.experimental import pallas as pl
from jax.sharding import Mesh, PartitionSpec as P
from jax.experimental.pallas import tpu as pltpu

VMEM = 63*2**20


def tables():
    x = np.arange(32); e = np.arange(8); b = np.arange(4)
    ka, kx = np.meshgrid(e, x, indexing="ij")
    xx, yh = np.meshgrid(x, e, indexing="ij")
    ph = (kx.reshape(-1,1)*xx.reshape(1,-1) + 4*ka.reshape(-1,1)*yh.reshape(1,-1)) % 32
    c, s = np.cos(2*np.pi*ph/32), np.sin(2*np.pi*ph/32)
    first = np.block([[c, s], [-s, c]])
    second = []
    kb, kz = np.meshgrid(b, x, indexing="ij")
    yl, z = np.meshgrid(b, x, indexing="ij")
    for a in range(8):
        ky = a + 8*kb.reshape(-1,1)
        ph = (kz.reshape(-1,1)*z.reshape(1,-1) + ky*yl.reshape(1,-1)) % 32
        second.append(np.concatenate([np.cos(2*np.pi*ph/32), np.sin(2*np.pi*ph/32)], 1))
    return first.astype(jnp.bfloat16), np.stack(second).astype(jnp.bfloat16)

def density_kernel(pos, place, val, con, first, second, scale, *rest):
    outs, (xs, yr, yi, zt, held) = rest[:8], rest[8:]
    v = pl.program_id(0)
    vr = val[v, 0].astype(jnp.float32)
    vi = val[v, 1].astype(jnp.float32)
    for pair in range(4):
        for k in range(2):
            cr = con[2*pair+k, 0].astype(jnp.float32)
            ci = con[2*pair+k, 1].astype(jnp.float32)
            xs[0:256, k*128:(k+1)*128] = (vr*cr + vi*ci).astype(jnp.bfloat16)
            xs[256:512, k*128:(k+1)*128] = (vr*ci - vi*cr).astype(jnp.bfloat16)
        y = jnp.dot(first[...], xs[...], preferred_element_type=jnp.float32)
        for k in range(2):
            p = v*8 + 2*pair + k
            yr[pl.ds(p, 256, stride=72), :] = y[0:256, k*128:(k+1)*128]
            yi[pl.ds(p, 256, stride=72), :] = y[256:512, k*128:(k+1)*128]

    @pl.when(v == 7)
    def _():
        def side(r):
            ar = yr[pl.ds(pl.multiple_of(r*72, 8), 64), :].astype(jnp.bfloat16)
            ai = yi[pl.ds(pl.multiple_of(r*72, 8), 64), :].astype(jnp.bfloat16)
            return [jnp.concatenate([ar, ai], 1), jnp.concatenate([ai, -ar], 1)]
        @pl.loop(0, 128, unroll=8)
        def _(q):
            r = q*2
            right = jnp.concatenate(side(r) + side(r+1), 0)
            z = lax.dot_general(second[r // 32], right, (((1,), (1,)), ((), ())), preferred_element_type=jnp.float32)
            zt[pl.ds(pl.multiple_of(r*128, 128), 128), :] = z[:, 0:128]
            zt[pl.ds(pl.multiple_of(r*128+128, 128), 128), :] = z[:, 128:256]
        w = scale[...]
        @pl.loop(0, 256, unroll=2)
        def _(q):
            rows = [zt[pl.ds(pos[q*16+j], 1), :] for j in range(16)]
            t = jnp.concatenate(rows, 0) * w
            held[pl.ds(pl.multiple_of(q*16, 16), 16), :] = t.astype(jnp.bfloat16)
        for s in range(4):
            a = lax.rem(place[0]+s, 4)*1024
            for q, shift in enumerate((2, 0, 1, 3)):
                to = lax.rem(place[2]+shift, 4)
                block = lax.rem(to, 2)*2 + lax.div(to, 2)
                outs[s][q*256:(q+1)*256, :] = held[pl.ds(pl.multiple_of(a + block*256, 256), 256), :]
            b = lax.rem(place[1]+s, 4)*1024
            for q in range(4):
                outs[4+s][:, q*256:(q+1)*256] = held[pl.ds(pl.multiple_of(b + q*256, 256), 256), :].T


def densities(pos, place, val, con, scale):
    first, second = tables()
    full = lambda shape: pl.BlockSpec(shape, lambda i, *_: (0,)*len(shape))
    return pl.pallas_call(
        density_kernel,
        grid_spec=pltpu.PrefetchScalarGridSpec(
            num_scalar_prefetch=2, grid=(8,),
            in_specs=[full((8,2,256,128)), full((8,2,256,128)), full((512,512)), full((8,128,256)), full((1,128))],
            out_specs=[full((1024,128))]*4 + [full((128,1024))]*4,
            scratch_shapes=[pltpu.VMEM((512,256), jnp.bfloat16), pltpu.VMEM((256*72,128), jnp.float32),
                pltpu.VMEM((256*72,128), jnp.float32), pltpu.VMEM((32768,128), jnp.float32), pltpu.VMEM((4096,128), jnp.bfloat16)],
        ),
        out_shape=[jax.ShapeDtypeStruct((1024,128), jnp.bfloat16)]*4 + [jax.ShapeDtypeStruct((128,1024), jnp.bfloat16)]*4,
        compiler_params=pltpu.CompilerParams(vmem_limit_bytes=VMEM),
        name="densities",
    )(pos, place, val, con, jnp.asarray(first), jnp.asarray(second), scale)


def product_kernel(place, *refs):
    rows, cols, refs = refs[0:4], refs[4:12], refs[12:]
    got, refs = (refs[:2], refs[2:]) if len(refs) == 14 else ((), refs)
    outs = refs[:-10]
    left, panel, come, ready, right0, right1, row_sem, col_sem, got_sem, out_sem = refs[-10:]
    right = (right0, right1)
    row_copies = [
        pltpu.make_async_copy(
            rows[t].at[s], left.at[:, pl.ds((t*4 + s)*128, 128)], row_sem.at[t, s])
        for t in range(4) for s in range(4)]
    col_copies = [
        pltpu.make_async_copy(cols[q], panel.at[q], col_sem.at[q]) for q in range(8)]
    got_copies = [pltpu.make_async_copy(got[h], come.at[h], got_sem.at[h]) for h in range(len(got))]
    for copy in col_copies[:4] + row_copies + col_copies[4:] + got_copies:
        copy.start()

    def fill(n):
        into, h = right[n % 2], n % 2
        for t in range(4):
            for s in range(4):
                k = (t*4 + s)*128
                piece = panel[4*(n//2) + s, t, :, h*256:(h+1)*256]
                into[k:k+128, 0:256] = piece
                into[k:k+64, 256:512] = -piece[64:128]
                into[k+64:k+128, 256:512] = piece[0:64]

    for copy in col_copies[:4]:
        copy.wait()
    fill(0)
    for copy in row_copies:
        copy.wait()
    leaving = []
    for n in range(4):
        if n == 1:
            for copy in col_copies[4:]:
                copy.wait()
        if n < 3:
            fill(n + 1)
        tile = jnp.dot(left[...], right[n % 2][...], preferred_element_type=jnp.float32)
        if n == 0:
            for copy in got_copies:
                copy.wait()
        h = n % 2
        side = place[0] + n//2 - 2*place[0]*(n//2)
        at = pl.multiple_of(side*256, 256)
        for o in range(2):
            one = tile[0:256, o*256:(o+1)*256]
            two = tile[256:512, o*256:(o+1)*256]
            if got:
                more = come[h, o, :, pl.ds(at, 256)].astype(jnp.float32)
                one, two = (one + more, two) if h == 0 else (one, two + more)
            ready[n, 0, o] = one.astype(jnp.bfloat16)
            ready[n, 1, o] = two.astype(jnp.bfloat16)
        wide = pl.ds(pl.multiple_of(h*512 + at, 256), 256)
        if got:
            first = outs[0].at[:, :, wide]
        else:
            first = outs[h].at[:, :, pl.ds(at, 256)]
        for b, to in enumerate((first, outs[-1].at[:, :, wide])):
            copy = pltpu.make_async_copy(ready.at[n, b], to, out_sem.at[n, b])
            copy.start()
            leaving.append(copy)
    for copy in leaving:
        copy.wait()


def product(place, rows, own, other, got):
    wide = jax.ShapeDtypeStruct((2, 256, 1024), jnp.bfloat16)
    slim = jax.ShapeDtypeStruct((2, 256, 512), jnp.bfloat16)
    shapes = [wide, wide] if got else [slim, slim, wide]
    anywhere = pl.BlockSpec(memory_space=pl.ANY)
    return pl.pallas_call(
        product_kernel,
        grid_spec=pltpu.PrefetchScalarGridSpec(
            num_scalar_prefetch=1, grid=(1,),
            in_specs=[anywhere]*(12 + len(got)),
            out_specs=[anywhere]*len(shapes),
            scratch_shapes=[
                pltpu.VMEM((512, 2048), jnp.bfloat16),
                pltpu.VMEM((8, 4, 128, 512), jnp.bfloat16),
                pltpu.VMEM((2, 2, 256, 512), jnp.bfloat16),
                pltpu.VMEM((4, 2, 2, 256, 256), jnp.bfloat16),
                pltpu.VMEM((2048, 512), jnp.bfloat16),
                pltpu.VMEM((2048, 512), jnp.bfloat16),
                pltpu.SemaphoreType.DMA((4, 4)),
                pltpu.SemaphoreType.DMA((8,)),
                pltpu.SemaphoreType.DMA((2,)),
                pltpu.SemaphoreType.DMA((4, 2)),
            ],
        ),
        out_shape=shapes,
        compiler_params=pltpu.CompilerParams(vmem_limit_bytes=VMEM),
        cost_estimate=pl.CostEstimate(flops=2**10, bytes_accessed=2**10, transcendentals=0),
        name="product",
    )(place, *rows, *own, *other, *got)


def total_kernel(a, b, c, *rest):
    out = rest[-1]
    t = a[...].astype(jnp.float32) + b[...].astype(jnp.float32) + c[...].astype(jnp.float32)
    out[:, 0, :] = t[0]
    out[:, 1, :] = t[1]


def total(parts, chunk, before):
    spec = pl.BlockSpec((2, 64, 1024), lambda n: (0, n, 0))
    more = [] if before is None else [before]
    return pl.pallas_call(
        total_kernel,
        grid=(4,),
        in_specs=[spec]*3 + [pl.BlockSpec(memory_space=pl.ANY)]*len(more),
        out_specs=pl.BlockSpec((64, 2, 1024), lambda n: (n, 0, chunk)),
        out_shape=jax.ShapeDtypeStruct((256, 2, 2048), jnp.float32),
        input_output_aliases={3: 0} if more else {},
        compiler_params=pltpu.CompilerParams(vmem_limit_bytes=VMEM),
        cost_estimate=pl.CostEstimate(flops=2**10, bytes_accessed=2**10, transcendentals=0),
        name="total",
    )(*parts, *more)


def ring(shift):
    return [(i, (i + shift) % 4) for i in range(4)]


def along_z(block, shift):
    place = lambda z: (z % 2)*2 + z//2
    return lax.ppermute(block, ("zl", "zh"), [(place(i), place((i + shift) % 4)) for i in range(4)])


def after(arrays, *first):
    return lax.optimization_barrier((tuple(arrays), first))[0]


def swapped(blocks):
    return [lax.ppermute(a, "core", [(0, 1), (1, 0)]) for a in blocks]


def local(valence_index, conduction_index, valence_waves, conduction_waves,
          valence_energy, conduction_energy, frequency, sphere_map):
    x, y = lax.axis_index("x"), lax.axis_index("y")
    zl, zh, core = lax.axis_index("zl"), lax.axis_index("zh"), lax.axis_index("core")
    vb, cb = (y*2 + zl)*8, (x*2 + zh)*8
    val = lax.dynamic_slice(valence_waves, (vb, 0, 0), (8, 2, 32768)).reshape(8, 2, 256, 128)
    con = lax.dynamic_slice(conduction_waves, (cb, 0, 0), (8, 2, 32768)).reshape(8, 2, 256, 128)
    channel = lax.iota(jnp.int32, 128)[:, None] % 64
    band = lax.iota(jnp.int32, 64)[None, :]
    gap = jnp.sum(
        jnp.where(band == cb + channel % 8, conduction_energy[None, :], 0.0)
        - jnp.where(band == vb + channel//8, valence_energy[None, :], 0.0), axis=1)
    weight = 4.0 * gap / (gap*gap + frequency[0]*frequency[0]) / 4096
    scale = jnp.sqrt(weight / 32768.0)[None, :]
    point = lax.dynamic_index_in_dim(sphere_map.reshape(16, 2, 256), core, 1, keepdims=False).reshape(4096)
    ky = (point >> 5) & 31
    pos = ((ky & 7)*32 + (point >> 10))*128 + (ky >> 3)*32 + (point & 31)
    place = jnp.stack([x, y, zh*2 + zl]).astype(jnp.int32)
    where = jnp.stack([core, x]).astype(jnp.int32)
    parts = densities(pos, place, val, con, scale)
    row = [parts[0]] + [None]*3
    col = [parts[4]] + [None]*3
    for s in (2, 1, 3):
        row[s] = lax.ppermute(parts[s], "x", ring(s))
        col[s] = lax.ppermute(parts[4 + s], "y", ring(s))
    row, col = jnp.stack(row), jnp.stack(col)
    row_a, col_a = row[:, :512], col[:, :, :512]
    row_b, col_b = row[:, 512:], col[:, :, 512:]
    rows_a, own_a = [row_a] + [None]*3, [col_a] + [None]*3
    for s in (1, 3):
        rows_a[s] = lax.ppermute(row_a, "y", ring(s))
        own_a[s] = lax.ppermute(col_a, "x", ring(s))
    rows_a[2] = lax.ppermute(row_a, "y", ring(2))
    col_a = after((col_a,), own_a[1], own_a[3])[0]
    own_a[2] = lax.ppermute(col_a, "x", ring(2))
    other_a = swapped(own_a)
    row_b, col_b = after((row_b, col_b), rows_a[2], own_a[2], other_a[0], other_a[1], other_a[3])
    rows_b, own_b = [row_b] + [None]*3, [col_b] + [None]*3
    for s in (1, 3):
        rows_b[s] = lax.ppermute(row_b, "y", ring(s))
        own_b[s] = lax.ppermute(col_b, "x", ring(s))
    own_b[2] = lax.ppermute(col_b, "x", ring(2))
    far0, far1, mine_a = product(where, rows_a, own_a, other_a, [])
    got_a = [along_z(far0, 1), along_z(far1, -1)]
    rows_b[2] = lax.ppermute(after((row_b,), far0, rows_b[1], rows_b[3])[0], "y", ring(2))
    other_b = swapped(after(own_b, far0))
    far0, far1, mine_b = product(where, rows_a, own_b, other_b, [])
    got_b = [along_z(far0, 1), along_z(far1, -1)]
    up_a, down_a = product(where, rows_b, own_a, other_a, got_a)
    done_a = [mine_a, along_z(up_a, 1), along_z(down_a, -1)]
    up_b, down_b = product(where, rows_b, own_b, other_b, got_b)
    done_b = [mine_b, along_z(up_b, 1), along_z(down_b, -1)]
    return total(done_b, 1, total(done_a, 0, None))


def solution(mesh):
    shaped = Mesh(mesh.devices.reshape(4, 2, 2, 2, 4), ("x", "zl", "zh", "core", "y"))
    split = P(("x", "zl", "zh", "core", "y"))
    return jax.shard_map(
        local,
        mesh=shaped,
        in_specs=(split, split, P(), P(), P(), P(), P(), P()),
        out_specs=P(("x", "zl", "zh", "core"), None, "y"),
        check_vma=False,
    )
```

```python
import numpy as np
import jax, jax.numpy as jnp
from jax import lax
from jax.experimental import pallas as pl
from jax.sharding import Mesh, PartitionSpec as P
from jax.experimental.pallas import tpu as pltpu

VMEM = 63*2**20


def tables():
    x = np.arange(32); e = np.arange(8); b = np.arange(4)
    ka, kx = np.meshgrid(e, x, indexing="ij")
    xx, yh = np.meshgrid(x, e, indexing="ij")
    ph = (kx.reshape(-1,1)*xx.reshape(1,-1) + 4*ka.reshape(-1,1)*yh.reshape(1,-1)) % 32
    c, s = np.cos(2*np.pi*ph/32), np.sin(2*np.pi*ph/32)
    first = np.block([[c, s], [-s, c]])
    second = []
    kb, kz = np.meshgrid(b, x, indexing="ij")
    yl, z = np.meshgrid(b, x, indexing="ij")
    for a in range(8):
        ky = a + 8*kb.reshape(-1,1)
        ph = (kz.reshape(-1,1)*z.reshape(1,-1) + ky*yl.reshape(1,-1)) % 32
        second.append(np.concatenate([np.cos(2*np.pi*ph/32), np.sin(2*np.pi*ph/32)], 1))
    return first.astype(jnp.bfloat16), np.stack(second).astype(jnp.bfloat16)

def density_kernel(pos, place, val, con, first, second, scale, *rest):
    outs, (xs, yr, yi, zt, held, turned, row_sem, col_sem) = rest[:8], rest[8:]
    v = pl.program_id(0)
    vr = val[v, 0].astype(jnp.float32)
    vi = val[v, 1].astype(jnp.float32)
    for pair in range(4):
        for k in range(2):
            cr = con[2*pair+k, 0].astype(jnp.float32)
            ci = con[2*pair+k, 1].astype(jnp.float32)
            xs[0:256, k*128:(k+1)*128] = (vr*cr + vi*ci).astype(jnp.bfloat16)
            xs[256:512, k*128:(k+1)*128] = (vr*ci - vi*cr).astype(jnp.bfloat16)
        y = jnp.dot(first[...], xs[...], preferred_element_type=jnp.float32)
        for k in range(2):
            p = v*8 + 2*pair + k
            yr[pl.ds(p, 256, stride=72), :] = y[0:256, k*128:(k+1)*128]
            yi[pl.ds(p, 256, stride=72), :] = y[256:512, k*128:(k+1)*128]

    @pl.when(v == 7)
    def _():
        def side(r):
            ar = yr[pl.ds(pl.multiple_of(r*72, 8), 64), :].astype(jnp.bfloat16)
            ai = yi[pl.ds(pl.multiple_of(r*72, 8), 64), :].astype(jnp.bfloat16)
            return [jnp.concatenate([ar, ai], 1), jnp.concatenate([ai, -ar], 1)]
        @pl.loop(0, 128, unroll=32)
        def _(q):
            r = q*2
            right = jnp.concatenate(side(r) + side(r+1), 0)
            z = lax.dot_general(second[r // 32], right, (((1,), (1,)), ((), ())), preferred_element_type=jnp.float32)
            zt[pl.ds(pl.multiple_of(r*128, 128), 128), :] = z[:, 0:128]
            zt[pl.ds(pl.multiple_of(r*128+128, 128), 128), :] = z[:, 128:256]
        w = scale[...]
        @pl.loop(0, 16)
        def _(block):
            base = (block*2 + place[3])*256

            @pl.loop(0, 16, unroll=4)
            def _(q):
                rows = [zt[pl.ds(pos[base + q*16 + j], 1), :] for j in range(16)]
                t = jnp.concatenate(rows, 0) * w
                held[pl.ds(pl.multiple_of(block*256 + q*16, 16), 16), :] = t.astype(jnp.bfloat16)

        leaving = []
        for s in range(4):
            a = lax.rem(place[0]+s, 4)*1024
            for q, shift in enumerate((2, 0, 1, 3)):
                to = lax.rem(place[2]+shift, 4)
                block = lax.rem(to, 2)*2 + lax.div(to, 2)
                copy = pltpu.make_async_copy(
                    held.at[pl.ds(pl.multiple_of(a + block*256, 256), 256), :],
                    outs[s].at[q*256:(q+1)*256, :], row_sem.at[s, q])
                copy.start()
                leaving.append(copy)
        for s in range(4):
            b = lax.rem(place[1]+s, 4)*1024
            for q in range(4):
                turned[s, :, q*256:(q+1)*256] = held[pl.ds(pl.multiple_of(b + q*256, 256), 256), :].T
            copy = pltpu.make_async_copy(turned.at[s], outs[4+s], col_sem.at[s])
            copy.start()
            leaving.append(copy)
        for copy in leaving:
            copy.wait()


def densities(pos, place, val, con, scale):
    first, second = tables()
    full = lambda shape: pl.BlockSpec(shape, lambda i, *_: (0,)*len(shape))
    return pl.pallas_call(
        density_kernel,
        grid_spec=pltpu.PrefetchScalarGridSpec(
            num_scalar_prefetch=2, grid=(8,),
            in_specs=[full((8,2,256,128)), full((8,2,256,128)), full((512,512)), full((8,128,256)), full((1,128))],
            out_specs=[pl.BlockSpec(memory_space=pl.ANY)]*8,
            scratch_shapes=[pltpu.VMEM((512,256), jnp.bfloat16), pltpu.VMEM((256*72,128), jnp.float32),
                pltpu.VMEM((256*72,128), jnp.float32), pltpu.VMEM((32768,128), jnp.float32), pltpu.VMEM((4096,128), jnp.bfloat16),
                pltpu.VMEM((4,128,1024), jnp.bfloat16), pltpu.SemaphoreType.DMA((4,4)), pltpu.SemaphoreType.DMA((4,))],
        ),
        out_shape=[jax.ShapeDtypeStruct((1024,128), jnp.bfloat16)]*4 + [jax.ShapeDtypeStruct((128,1024), jnp.bfloat16)]*4,
        compiler_params=pltpu.CompilerParams(vmem_limit_bytes=VMEM),
        name="densities",
    )(pos, place, val, con, jnp.asarray(first), jnp.asarray(second), scale)


def product_kernel(place, *refs):
    rows, cols, refs = refs[0:4], refs[4:12], refs[12:]
    got, refs = (refs[:2], refs[2:]) if len(refs) == 14 else ((), refs)
    outs = refs[:-10]
    left, panel, come, ready, right0, right1, row_sem, col_sem, got_sem, out_sem = refs[-10:]
    right = (right0, right1)
    row_copies = [
        pltpu.make_async_copy(
            rows[t].at[s], left.at[:, pl.ds((t*4 + s)*128, 128)], row_sem.at[t, s])
        for t in range(4) for s in range(4)]
    col_copies = [
        pltpu.make_async_copy(cols[q], panel.at[q], col_sem.at[q]) for q in range(8)]
    got_copies = [pltpu.make_async_copy(got[h], come.at[h], got_sem.at[h]) for h in range(len(got))]
    for copy in col_copies[:4] + row_copies + col_copies[4:] + got_copies:
        copy.start()

    def fill(n):
        into, h = right[n % 2], n % 2
        for t in range(4):
            for s in range(4):
                k = (t*4 + s)*128
                piece = panel[4*(n//2) + s, t, :, h*256:(h+1)*256]
                into[k:k+128, 0:256] = piece
                into[k:k+64, 256:512] = -piece[64:128]
                into[k+64:k+128, 256:512] = piece[0:64]

    for copy in col_copies[:4]:
        copy.wait()
    fill(0)
    for copy in row_copies:
        copy.wait()
    leaving = []
    for n in range(4):
        if n == 1:
            for copy in col_copies[4:]:
                copy.wait()
        if n < 3:
            fill(n + 1)
        tile = jnp.dot(left[...], right[n % 2][...], preferred_element_type=jnp.float32)
        if n == 0:
            for copy in got_copies:
                copy.wait()
        h = n % 2
        side = place[3] + n//2 - 2*place[3]*(n//2)
        at = pl.multiple_of(side*256, 256)
        for o in range(2):
            one = tile[0:256, o*256:(o+1)*256]
            two = tile[256:512, o*256:(o+1)*256]
            if got:
                more = come[h, o, :, pl.ds(at, 256)].astype(jnp.float32)
                one, two = (one + more, two) if h == 0 else (one, two + more)
            ready[n, 0, o] = one.astype(jnp.bfloat16)
            ready[n, 1, o] = two.astype(jnp.bfloat16)
        wide = pl.ds(pl.multiple_of(h*512 + at, 256), 256)
        if got:
            first = outs[0].at[:, :, wide]
        else:
            first = outs[h].at[:, :, pl.ds(at, 256)]
        for b, to in enumerate((first, outs[-1].at[:, :, wide])):
            copy = pltpu.make_async_copy(ready.at[n, b], to, out_sem.at[n, b])
            copy.start()
            leaving.append(copy)
    for copy in leaving:
        copy.wait()


def product(place, rows, own, other, got):
    wide = jax.ShapeDtypeStruct((2, 256, 1024), jnp.bfloat16)
    slim = jax.ShapeDtypeStruct((2, 256, 512), jnp.bfloat16)
    shapes = [wide, wide] if got else [slim, slim, wide]
    anywhere = pl.BlockSpec(memory_space=pl.ANY)
    return pl.pallas_call(
        product_kernel,
        grid_spec=pltpu.PrefetchScalarGridSpec(
            num_scalar_prefetch=1, grid=(1,),
            in_specs=[anywhere]*(12 + len(got)),
            out_specs=[anywhere]*len(shapes),
            scratch_shapes=[
                pltpu.VMEM((512, 2048), jnp.bfloat16),
                pltpu.VMEM((8, 4, 128, 512), jnp.bfloat16),
                pltpu.VMEM((2, 2, 256, 512), jnp.bfloat16),
                pltpu.VMEM((4, 2, 2, 256, 256), jnp.bfloat16),
                pltpu.VMEM((2048, 512), jnp.bfloat16),
                pltpu.VMEM((2048, 512), jnp.bfloat16),
                pltpu.SemaphoreType.DMA((4, 4)),
                pltpu.SemaphoreType.DMA((8,)),
                pltpu.SemaphoreType.DMA((2,)),
                pltpu.SemaphoreType.DMA((4, 2)),
            ],
        ),
        out_shape=shapes,
        compiler_params=pltpu.CompilerParams(vmem_limit_bytes=VMEM),
        cost_estimate=pl.CostEstimate(flops=2**10, bytes_accessed=2**10, transcendentals=0),
        name="product",
    )(place, *rows, *own, *other, *got)


def total_kernel(a, b, c, *rest):
    out = rest[-1]
    t = a[...].astype(jnp.float32) + b[...].astype(jnp.float32) + c[...].astype(jnp.float32)
    out[:, 0, :] = t[0]
    out[:, 1, :] = t[1]


def total(parts, chunk, before):
    spec = pl.BlockSpec((2, 128, 1024), lambda n: (0, n, 0))
    more = [] if before is None else [before]
    return pl.pallas_call(
        total_kernel,
        grid=(2,),
        in_specs=[spec]*3 + [pl.BlockSpec(memory_space=pl.ANY)]*len(more),
        out_specs=pl.BlockSpec((128, 2, 1024), lambda n: (n, 0, chunk)),
        out_shape=jax.ShapeDtypeStruct((256, 2, 2048), jnp.float32),
        input_output_aliases={3: 0} if more else {},
        compiler_params=pltpu.CompilerParams(vmem_limit_bytes=VMEM),
        cost_estimate=pl.CostEstimate(flops=2**10, bytes_accessed=2**10, transcendentals=0),
        name="total",
    )(*parts, *more)


def ring(shift):
    return [(i, (i + shift) % 4) for i in range(4)]


def along_z(block, shift):
    place = lambda z: (z % 2)*2 + z//2
    return lax.ppermute(block, ("zl", "zh"), [(place(i), place((i + shift) % 4)) for i in range(4)])


def after(arrays, *first):
    return lax.optimization_barrier((tuple(arrays), first))[0]


def swapped(blocks):
    return [lax.ppermute(a, "core", [(0, 1), (1, 0)]) for a in blocks]


def local(valence_index, conduction_index, valence_waves, conduction_waves,
          valence_energy, conduction_energy, frequency, sphere_map):
    x, y = lax.axis_index("x"), lax.axis_index("y")
    zl, zh, core = lax.axis_index("zl"), lax.axis_index("zh"), lax.axis_index("core")
    vb, cb = (y*2 + zl)*8, (x*2 + zh)*8
    val = lax.dynamic_slice(valence_waves, (vb, 0, 0), (8, 2, 32768)).reshape(8, 2, 256, 128)
    con = lax.dynamic_slice(conduction_waves, (cb, 0, 0), (8, 2, 32768)).reshape(8, 2, 256, 128)
    channel = lax.iota(jnp.int32, 128)[:, None] % 64
    band = lax.iota(jnp.int32, 64)[None, :]
    gap = jnp.sum(
        jnp.where(band == cb + channel % 8, conduction_energy[None, :], 0.0)
        - jnp.where(band == vb + channel//8, valence_energy[None, :], 0.0), axis=1)
    weight = 4.0 * gap / (gap*gap + frequency[0]*frequency[0]) / 4096
    scale = jnp.sqrt(weight / 32768.0)[None, :]
    ky = (sphere_map >> 5) & 31
    pos = ((ky & 7)*32 + (sphere_map >> 10))*128 + (ky >> 3)*32 + (sphere_map & 31)
    where = jnp.stack([x, y, zh*2 + zl, core]).astype(jnp.int32)
    parts = densities(pos, where, val, con, scale)
    row = [parts[0]] + [None]*3
    col = [parts[4]] + [None]*3
    for s in (2, 1, 3):
        row[s] = lax.ppermute(parts[s], "x", ring(s))
        col[s] = lax.ppermute(parts[4 + s], "y", ring(s))
    row_a, col_a = jnp.stack([r[:512] for r in row]), jnp.stack([c[:, :512] for c in col])
    row_b, col_b = jnp.stack([r[512:] for r in row]), jnp.stack([c[:, 512:] for c in col])
    rows_a, own_a = [row_a] + [None]*3, [col_a] + [None]*3
    for s in (1, 3):
        rows_a[s] = lax.ppermute(row_a, "y", ring(s))
        own_a[s] = lax.ppermute(col_a, "x", ring(s))
    rows_a[2] = lax.ppermute(row_a, "y", ring(2))
    col_a = after((col_a,), own_a[1], own_a[3])[0]
    own_a[2] = lax.ppermute(col_a, "x", ring(2))
    other_a = swapped(own_a)
    row_b, col_b = after((row_b, col_b), rows_a[2], own_a[2], other_a[0], other_a[1], other_a[3])
    rows_b, own_b = [row_b] + [None]*3, [col_b] + [None]*3
    for s in (1, 3):
        rows_b[s] = lax.ppermute(row_b, "y", ring(s))
        own_b[s] = lax.ppermute(col_b, "x", ring(s))
    own_b[2] = lax.ppermute(col_b, "x", ring(2))
    far0, far1, mine_a = product(where, rows_a, own_a, other_a, [])
    got_a = [along_z(far0, 1), along_z(far1, -1)]
    rows_b[2] = lax.ppermute(after((row_b,), far0, rows_b[1], rows_b[3])[0], "y", ring(2))
    other_b = swapped(after(own_b, far0))
    far0, far1, mine_b = product(where, rows_a, own_b, other_b, [])
    got_b = [along_z(far0, 1), along_z(far1, -1)]
    up_a, down_a = product(where, rows_b, own_a, other_a, got_a)
    done_a = [mine_a, along_z(up_a, 1), along_z(down_a, -1)]
    up_b, down_b = product(where, rows_b, own_b, other_b, got_b)
    done_b = [mine_b, along_z(up_b, 1), along_z(down_b, -1)]
    return total(done_b, 1, total(done_a, 0, None))


def solution(mesh):
    shaped = Mesh(mesh.devices.reshape(4, 2, 2, 2, 4), ("x", "zl", "zh", "core", "y"))
    split = P(("x", "zl", "zh", "core", "y"))
    return jax.shard_map(
        local,
        mesh=shaped,
        in_specs=(split, split, P(), P(), P(), P(), P(), P()),
        out_specs=P(("x", "zl", "zh", "core"), None, "y"),
        check_vma=False,
    )
```

```python
import numpy as np
import jax, jax.numpy as jnp
from jax import lax
from jax.experimental import pallas as pl
from jax.sharding import Mesh, PartitionSpec as P
from jax.experimental.pallas import tpu as pltpu

VMEM = 63*2**20


def tables():
    x = np.arange(32); e = np.arange(8); b = np.arange(4)
    ka, kx = np.meshgrid(e, x, indexing="ij")
    xx, yh = np.meshgrid(x, e, indexing="ij")
    ph = (kx.reshape(-1,1)*xx.reshape(1,-1) + 4*ka.reshape(-1,1)*yh.reshape(1,-1)) % 32
    c, s = np.cos(2*np.pi*ph/32), np.sin(2*np.pi*ph/32)
    first = np.block([[c, s], [-s, c]])
    second = []
    kb, kz = np.meshgrid(b, x, indexing="ij")
    yl, z = np.meshgrid(b, x, indexing="ij")
    for a in range(8):
        ky = a + 8*kb.reshape(-1,1)
        ph = (kz.reshape(-1,1)*z.reshape(1,-1) + ky*yl.reshape(1,-1)) % 32
        second.append(np.concatenate([np.cos(2*np.pi*ph/32), np.sin(2*np.pi*ph/32)], 1))
    return first.astype(jnp.bfloat16), np.stack(second).astype(jnp.bfloat16)

def density_kernel(pos, place, val, con, first, second, scale, *rest):
    outs, (xs, yr, yi, zt, held, turned, row_sem, col_sem) = rest[:8], rest[8:]
    step = pl.program_id(0)
    for v in (2*step, 2*step + 1):
        vr = val[v, 0].astype(jnp.float32)
        vi = val[v, 1].astype(jnp.float32)
        for pair in range(4):
            for k in range(2):
                cr = con[2*pair+k, 0].astype(jnp.float32)
                ci = con[2*pair+k, 1].astype(jnp.float32)
                xs[0:256, k*128:(k+1)*128] = (vr*cr + vi*ci).astype(jnp.bfloat16)
                xs[256:512, k*128:(k+1)*128] = (vr*ci - vi*cr).astype(jnp.bfloat16)
            y = jnp.dot(first[...], xs[...], preferred_element_type=jnp.float32)
            for k in range(2):
                p = v*8 + 2*pair + k
                yr[pl.ds(p, 256, stride=72), :] = y[0:256, k*128:(k+1)*128]
                yi[pl.ds(p, 256, stride=72), :] = y[256:512, k*128:(k+1)*128]

    @pl.when(step == 3)
    def _():
        def side(r):
            ar = yr[pl.ds(pl.multiple_of(r*72, 8), 64), :].astype(jnp.bfloat16)
            ai = yi[pl.ds(pl.multiple_of(r*72, 8), 64), :].astype(jnp.bfloat16)
            return [jnp.concatenate([ar, ai], 1), jnp.concatenate([ai, -ar], 1)]
        @pl.loop(0, 128, unroll=32)
        def _(q):
            r = q*2
            right = jnp.concatenate(side(r) + side(r+1), 0)
            z = lax.dot_general(second[r // 32], right, (((1,), (1,)), ((), ())), preferred_element_type=jnp.float32)
            zt[pl.ds(pl.multiple_of(r*128, 128), 128), :] = z[:, 0:128]
            zt[pl.ds(pl.multiple_of(r*128+128, 128), 128), :] = z[:, 128:256]
        w = scale[...]
        @pl.loop(0, 16)
        def _(block):
            base = (block*2 + place[3])*256

            @pl.loop(0, 16, unroll=4)
            def _(q):
                rows = [zt[pl.ds(pos[base + q*16 + j], 1), :] for j in range(16)]
                t = jnp.concatenate(rows, 0) * w
                held[pl.ds(pl.multiple_of(block*256 + q*16, 16), 16), :] = t.astype(jnp.bfloat16)

        leaving = []
        for s in range(4):
            a = lax.rem(place[0]+s, 4)*1024
            for q, shift in enumerate((2, 0, 1, 3)):
                to = lax.rem(place[2]+shift, 4)
                block = lax.rem(to, 2)*2 + lax.div(to, 2)
                copy = pltpu.make_async_copy(
                    held.at[pl.ds(pl.multiple_of(a + block*256, 256), 256), :],
                    outs[s].at[q*256:(q+1)*256, :], row_sem.at[s, q])
                copy.start()
                leaving.append(copy)
        for s in range(4):
            b = lax.rem(place[1]+s, 4)*1024
            for q in range(4):
                turned[s, :, q*256:(q+1)*256] = held[pl.ds(pl.multiple_of(b + q*256, 256), 256), :].T
            copy = pltpu.make_async_copy(turned.at[s], outs[4+s], col_sem.at[s])
            copy.start()
            leaving.append(copy)
        for copy in leaving:
            copy.wait()


def densities(pos, place, val, con, scale):
    first, second = tables()
    full = lambda shape: pl.BlockSpec(shape, lambda i, *_: (0,)*len(shape))
    return pl.pallas_call(
        density_kernel,
        grid_spec=pltpu.PrefetchScalarGridSpec(
            num_scalar_prefetch=2, grid=(4,),
            in_specs=[full((8,2,256,128)), full((8,2,256,128)), full((512,512)), full((8,128,256)), full((1,128))],
            out_specs=[pl.BlockSpec(memory_space=pl.ANY)]*8,
            scratch_shapes=[pltpu.VMEM((512,256), jnp.bfloat16), pltpu.VMEM((256*72,128), jnp.float32),
                pltpu.VMEM((256*72,128), jnp.float32), pltpu.VMEM((32768,128), jnp.float32), pltpu.VMEM((4096,128), jnp.bfloat16),
                pltpu.VMEM((4,128,1024), jnp.bfloat16), pltpu.SemaphoreType.DMA((4,4)), pltpu.SemaphoreType.DMA((4,))],
        ),
        out_shape=[jax.ShapeDtypeStruct((1024,128), jnp.bfloat16)]*4 + [jax.ShapeDtypeStruct((128,1024), jnp.bfloat16)]*4,
        compiler_params=pltpu.CompilerParams(vmem_limit_bytes=50*2**20),
        name="densities",
    )(pos, place, val, con, jnp.asarray(first), jnp.asarray(second), scale)


def product_kernel(place, *refs):
    rows, cols, refs = refs[0:4], refs[4:12], refs[12:]
    got, refs = (refs[:2], refs[2:]) if len(refs) == 14 else ((), refs)
    outs = refs[:-10]
    left, panel, come, ready, right0, right1, row_sem, col_sem, got_sem, out_sem = refs[-10:]
    right = (right0, right1)
    row_copies = [
        pltpu.make_async_copy(
            rows[t].at[s], left.at[:, pl.ds((t*4 + s)*128, 128)], row_sem.at[t, s])
        for t in range(4) for s in range(4)]
    col_copies = [
        pltpu.make_async_copy(cols[q], panel.at[q], col_sem.at[q]) for q in range(8)]
    got_copies = [pltpu.make_async_copy(got[h], come.at[h], got_sem.at[h]) for h in range(len(got))]
    for copy in col_copies[:4] + row_copies + col_copies[4:] + got_copies:
        copy.start()

    def fill(n):
        into, h = right[n % 2], n % 2
        for t in range(4):
            for s in range(4):
                k = (t*4 + s)*128
                piece = panel[4*(n//2) + s, t, :, h*256:(h+1)*256]
                into[k:k+128, 0:256] = piece
                into[k:k+64, 256:512] = -piece[64:128]
                into[k+64:k+128, 256:512] = piece[0:64]

    for copy in col_copies[:4]:
        copy.wait()
    fill(0)
    for copy in row_copies:
        copy.wait()
    leaving = []
    for n in range(4):
        if n == 1:
            for copy in col_copies[4:]:
                copy.wait()
        if n < 3:
            fill(n + 1)
        tile = jnp.dot(left[...], right[n % 2][...], preferred_element_type=jnp.float32)
        if n == 0:
            for copy in got_copies:
                copy.wait()
        h = n % 2
        side = place[3] + n//2 - 2*place[3]*(n//2)
        at = pl.multiple_of(side*256, 256)
        for o in range(2):
            one = tile[0:256, o*256:(o+1)*256]
            two = tile[256:512, o*256:(o+1)*256]
            if got:
                more = come[h, o, :, pl.ds(at, 256)].astype(jnp.float32)
                one, two = (one + more, two) if h == 0 else (one, two + more)
            ready[n, 0, o] = one.astype(jnp.bfloat16)
            ready[n, 1, o] = two.astype(jnp.bfloat16)
        wide = pl.ds(pl.multiple_of(h*512 + at, 256), 256)
        if got:
            first = outs[0].at[:, :, wide]
        else:
            first = outs[h].at[:, :, pl.ds(at, 256)]
        for b, to in enumerate((first, outs[-1].at[:, :, wide])):
            copy = pltpu.make_async_copy(ready.at[n, b], to, out_sem.at[n, b])
            copy.start()
            leaving.append(copy)
    for copy in leaving:
        copy.wait()


def product(place, rows, own, other, got):
    wide = jax.ShapeDtypeStruct((2, 256, 1024), jnp.bfloat16)
    slim = jax.ShapeDtypeStruct((2, 256, 512), jnp.bfloat16)
    shapes = [wide, wide] if got else [slim, slim, wide]
    anywhere = pl.BlockSpec(memory_space=pl.ANY)
    return pl.pallas_call(
        product_kernel,
        grid_spec=pltpu.PrefetchScalarGridSpec(
            num_scalar_prefetch=1, grid=(1,),
            in_specs=[anywhere]*(12 + len(got)),
            out_specs=[anywhere]*len(shapes),
            scratch_shapes=[
                pltpu.VMEM((512, 2048), jnp.bfloat16),
                pltpu.VMEM((8, 4, 128, 512), jnp.bfloat16),
                pltpu.VMEM((2, 2, 256, 512), jnp.bfloat16),
                pltpu.VMEM((4, 2, 2, 256, 256), jnp.bfloat16),
                pltpu.VMEM((2048, 512), jnp.bfloat16),
                pltpu.VMEM((2048, 512), jnp.bfloat16),
                pltpu.SemaphoreType.DMA((4, 4)),
                pltpu.SemaphoreType.DMA((8,)),
                pltpu.SemaphoreType.DMA((2,)),
                pltpu.SemaphoreType.DMA((4, 2)),
            ],
        ),
        out_shape=shapes,
        compiler_params=pltpu.CompilerParams(vmem_limit_bytes=VMEM),
        cost_estimate=pl.CostEstimate(flops=2**10, bytes_accessed=2**10, transcendentals=0),
        name="product",
    )(place, *rows, *own, *other, *got)


def total_kernel(a, b, c, *rest):
    out = rest[-1]
    t = a[...].astype(jnp.float32) + b[...].astype(jnp.float32) + c[...].astype(jnp.float32)
    out[:, 0, :] = t[0]
    out[:, 1, :] = t[1]


def total(parts, chunk, before):
    spec = pl.BlockSpec((2, 128, 1024), lambda n: (0, n, 0))
    more = [] if before is None else [before]
    return pl.pallas_call(
        total_kernel,
        grid=(2,),
        in_specs=[spec]*3 + [pl.BlockSpec(memory_space=pl.ANY)]*len(more),
        out_specs=pl.BlockSpec((128, 2, 1024), lambda n: (n, 0, chunk)),
        out_shape=jax.ShapeDtypeStruct((256, 2, 2048), jnp.float32),
        input_output_aliases={3: 0} if more else {},
        compiler_params=pltpu.CompilerParams(vmem_limit_bytes=VMEM),
        cost_estimate=pl.CostEstimate(flops=2**10, bytes_accessed=2**10, transcendentals=0),
        name="total",
    )(*parts, *more)


def ring(shift):
    return [(i, (i + shift) % 4) for i in range(4)]


def along_z(block, shift):
    place = lambda z: (z % 2)*2 + z//2
    return lax.ppermute(block, ("zl", "zh"), [(place(i), place((i + shift) % 4)) for i in range(4)])


def after(arrays, *first):
    return lax.optimization_barrier((tuple(arrays), first))[0]


def swapped(blocks):
    return [lax.ppermute(a, "core", [(0, 1), (1, 0)]) for a in blocks]


def local(valence_index, conduction_index, valence_waves, conduction_waves,
          valence_energy, conduction_energy, frequency, sphere_map):
    x, y = lax.axis_index("x"), lax.axis_index("y")
    zl, zh, core = lax.axis_index("zl"), lax.axis_index("zh"), lax.axis_index("core")
    vb, cb = (y*2 + zl)*8, (x*2 + zh)*8
    val = lax.dynamic_slice(valence_waves, (vb, 0, 0), (8, 2, 32768)).reshape(8, 2, 256, 128)
    con = lax.dynamic_slice(conduction_waves, (cb, 0, 0), (8, 2, 32768)).reshape(8, 2, 256, 128)
    channel = lax.iota(jnp.int32, 128)[:, None] % 64
    band = lax.iota(jnp.int32, 64)[None, :]
    gap = jnp.sum(
        jnp.where(band == cb + channel % 8, conduction_energy[None, :], 0.0)
        - jnp.where(band == vb + channel//8, valence_energy[None, :], 0.0), axis=1)
    weight = 4.0 * gap / (gap*gap + frequency[0]*frequency[0]) / 4096
    scale = jnp.sqrt(weight / 32768.0)[None, :]
    ky = (sphere_map >> 5) & 31
    pos = ((ky & 7)*32 + (sphere_map >> 10))*128 + (ky >> 3)*32 + (sphere_map & 31)
    where = jnp.stack([x, y, zh*2 + zl, core]).astype(jnp.int32)
    parts = densities(pos, where, val, con, scale)
    row = [parts[0]] + [None]*3
    col = [parts[4]] + [None]*3
    for s in (2, 1, 3):
        row[s] = lax.ppermute(parts[s], "x", ring(s))
        col[s] = lax.ppermute(parts[4 + s], "y", ring(s))
    row_a, col_a = jnp.stack([r[:512] for r in row]), jnp.stack([c[:, :512] for c in col])
    row_b, col_b = jnp.stack([r[512:] for r in row]), jnp.stack([c[:, 512:] for c in col])
    rows_a, own_a = [row_a] + [None]*3, [col_a] + [None]*3
    for s in (1, 3):
        rows_a[s] = lax.ppermute(row_a, "y", ring(s))
        own_a[s] = lax.ppermute(col_a, "x", ring(s))
    rows_a[2] = lax.ppermute(row_a, "y", ring(2))
    col_a = after((col_a,), own_a[1], own_a[3])[0]
    own_a[2] = lax.ppermute(col_a, "x", ring(2))
    other_a = swapped(own_a)
    row_b, col_b = after((row_b, col_b), rows_a[2], own_a[2], other_a[0], other_a[1], other_a[3])
    rows_b, own_b = [row_b] + [None]*3, [col_b] + [None]*3
    for s in (1, 3):
        rows_b[s] = lax.ppermute(row_b, "y", ring(s))
        own_b[s] = lax.ppermute(col_b, "x", ring(s))
    own_b[2] = lax.ppermute(col_b, "x", ring(2))
    far0, far1, mine_a = product(where, rows_a, own_a, other_a, [])
    got_a = [along_z(far0, 1), along_z(far1, -1)]
    rows_b[2] = lax.ppermute(after((row_b,), far0, rows_b[1], rows_b[3])[0], "y", ring(2))
    other_b = swapped(after(own_b, far0))
    far0, far1, mine_b = product(where, rows_a, own_b, other_b, [])
    got_b = [along_z(far0, 1), along_z(far1, -1)]
    up_a, down_a = product(where, rows_b, own_a, other_a, got_a)
    done_a = [mine_a, along_z(up_a, 1), along_z(down_a, -1)]
    up_b, down_b = product(where, rows_b, own_b, other_b, got_b)
    done_b = [mine_b, along_z(up_b, 1), along_z(down_b, -1)]
    return total(done_b, 1, total(done_a, 0, None))


def solution(mesh):
    shaped = Mesh(mesh.devices.reshape(4, 2, 2, 2, 4), ("x", "zl", "zh", "core", "y"))
    split = P(("x", "zl", "zh", "core", "y"))
    return jax.shard_map(
        local,
        mesh=shaped,
        in_specs=(split, split, P(), P(), P(), P(), P(), P()),
        out_specs=P(("x", "zl", "zh", "core"), None, "y"),
        check_vma=False,
    )
```

```python
import numpy as np
import jax, jax.numpy as jnp
from jax import lax
from jax.experimental import pallas as pl
from jax.sharding import Mesh, PartitionSpec as P
from jax.experimental.pallas import tpu as pltpu

VMEM = 63*2**20


def tables():
    x = np.arange(32); e = np.arange(8); b = np.arange(4)
    ka, kx = np.meshgrid(e, x, indexing="ij")
    xx, yh = np.meshgrid(x, e, indexing="ij")
    ph = (kx.reshape(-1,1)*xx.reshape(1,-1) + 4*ka.reshape(-1,1)*yh.reshape(1,-1)) % 32
    c, s = np.cos(2*np.pi*ph/32), np.sin(2*np.pi*ph/32)
    first = np.block([[c, s], [-s, c]])
    second = []
    kb, kz = np.meshgrid(b, x, indexing="ij")
    yl, z = np.meshgrid(b, x, indexing="ij")
    for a in range(8):
        ky = a + 8*kb.reshape(-1,1)
        ph = (kz.reshape(-1,1)*z.reshape(1,-1) + ky*yl.reshape(1,-1)) % 32
        second.append(np.concatenate([np.cos(2*np.pi*ph/32), np.sin(2*np.pi*ph/32)], 1))
    return first.astype(jnp.bfloat16), np.stack(second).astype(jnp.bfloat16)

def density_kernel(pos, place, val, con, first, second, scale, *rest):
    outs, (xs, yr, yi, zt, held, turned, row_sem, col_sem) = rest[:8], rest[8:]
    step = pl.program_id(0)
    for v in (2*step, 2*step + 1):
        vr = val[v, 0].astype(jnp.float32)
        vi = val[v, 1].astype(jnp.float32)
        for pair in range(4):
            for k in range(2):
                cr = con[2*pair+k, 0].astype(jnp.float32)
                ci = con[2*pair+k, 1].astype(jnp.float32)
                xs[0:256, k*128:(k+1)*128] = (vr*cr + vi*ci).astype(jnp.bfloat16)
                xs[256:512, k*128:(k+1)*128] = (vr*ci - vi*cr).astype(jnp.bfloat16)
            y = jnp.dot(first[...], xs[...], preferred_element_type=jnp.float32)
            for k in range(2):
                p = v*8 + 2*pair + k
                yr[pl.ds(p, 256, stride=72), :] = y[0:256, k*128:(k+1)*128]
                yi[pl.ds(p, 256, stride=72), :] = y[256:512, k*128:(k+1)*128]

    @pl.when(step == 3)
    def _():
        def side(r):
            ar = yr[pl.ds(pl.multiple_of(r*72, 8), 64), :].astype(jnp.bfloat16)
            ai = yi[pl.ds(pl.multiple_of(r*72, 8), 64), :].astype(jnp.bfloat16)
            return [jnp.concatenate([ar, ai], 1), jnp.concatenate([ai, -ar], 1)]
        @pl.loop(0, 128, unroll=32)
        def _(q):
            r = q*2
            right = jnp.concatenate(side(r) + side(r+1), 0)
            z = lax.dot_general(second[r // 32], right, (((1,), (1,)), ((), ())), preferred_element_type=jnp.float32)
            zt[pl.ds(pl.multiple_of(r*128, 128), 128), :] = z[:, 0:128]
            zt[pl.ds(pl.multiple_of(r*128+128, 128), 128), :] = z[:, 128:256]
        w = scale[...]
        @pl.loop(0, 16)
        def _(block):
            base = (block*2 + place[3])*256

            @pl.loop(0, 16, unroll=4)
            def _(q):
                rows = [zt[pl.ds(pos[base + q*16 + j], 1), :] for j in range(16)]
                t = jnp.concatenate(rows, 0) * w
                held[pl.ds(pl.multiple_of(block*256 + q*16, 16), 16), :] = t.astype(jnp.bfloat16)

        leaving = []
        for s in range(4):
            a = lax.rem(place[0]+s, 4)*1024
            for q, shift in enumerate((2, 0, 1, 3)):
                to = lax.rem(place[2]+shift, 4)
                block = lax.rem(to, 2)*2 + lax.div(to, 2)
                copy = pltpu.make_async_copy(
                    held.at[pl.ds(pl.multiple_of(a + block*256, 256), 256), :],
                    outs[s].at[q*256:(q+1)*256, :], row_sem.at[s, q])
                copy.start()
                leaving.append(copy)
        for s in range(4):
            b = lax.rem(place[1]+s, 4)*1024
            for q in range(4):
                turned[s, :, q*256:(q+1)*256] = held[pl.ds(pl.multiple_of(b + q*256, 256), 256), :].T
            copy = pltpu.make_async_copy(turned.at[s], outs[4+s], col_sem.at[s])
            copy.start()
            leaving.append(copy)
        for copy in leaving:
            copy.wait()


def densities(pos, place, val, con, scale):
    first, second = tables()
    full = lambda shape: pl.BlockSpec(shape, lambda i, *_: (0,)*len(shape))
    return pl.pallas_call(
        density_kernel,
        grid_spec=pltpu.PrefetchScalarGridSpec(
            num_scalar_prefetch=2, grid=(4,),
            in_specs=[full((8,2,256,128)), full((8,2,256,128)), full((512,512)), full((8,128,256)), full((1,128))],
            out_specs=[pl.BlockSpec(memory_space=pl.ANY)]*8,
            scratch_shapes=[pltpu.VMEM((512,256), jnp.bfloat16), pltpu.VMEM((256*72,128), jnp.float32),
                pltpu.VMEM((256*72,128), jnp.float32), pltpu.VMEM((32768,128), jnp.float32), pltpu.VMEM((4096,128), jnp.bfloat16),
                pltpu.VMEM((4,128,1024), jnp.bfloat16), pltpu.SemaphoreType.DMA((4,4)), pltpu.SemaphoreType.DMA((4,))],
        ),
        out_shape=[jax.ShapeDtypeStruct((1024,128), jnp.bfloat16)]*4 + [jax.ShapeDtypeStruct((128,1024), jnp.bfloat16)]*4,
        compiler_params=pltpu.CompilerParams(vmem_limit_bytes=50*2**20),
        name="densities",
    )(pos, place, val, con, jnp.asarray(first), jnp.asarray(second), scale)


def product_kernel(place, *refs):
    rows, cols, refs = refs[0:4], refs[4:12], refs[12:]
    got, refs = (refs[:2], refs[2:]) if len(refs) == 14 else ((), refs)
    outs = refs[:-10]
    left, panel, come, ready, right0, right1, row_sem, col_sem, got_sem, out_sem = refs[-10:]
    right = (right0, right1)
    row_copies = [
        pltpu.make_async_copy(
            rows[t].at[s], left.at[:, pl.ds((t*4 + s)*128, 128)], row_sem.at[t, s])
        for t in range(4) for s in range(4)]
    col_copies = [
        pltpu.make_async_copy(cols[q], panel.at[q], col_sem.at[q]) for q in range(8)]
    got_copies = [pltpu.make_async_copy(got[h], come.at[h], got_sem.at[h]) for h in range(len(got))]
    for copy in col_copies[:4] + row_copies + col_copies[4:] + got_copies:
        copy.start()

    def fill(n):
        into, h = right[n % 2], n % 2
        for t in range(4):
            for s in range(4):
                k = (t*4 + s)*128
                piece = panel[4*(n//2) + s, t, :, h*256:(h+1)*256]
                into[k:k+128, 0:256] = piece
                into[k:k+64, 256:512] = -piece[64:128]
                into[k+64:k+128, 256:512] = piece[0:64]

    for copy in col_copies[:4]:
        copy.wait()
    fill(0)
    for copy in row_copies:
        copy.wait()
    leaving = []
    for n in range(4):
        if n == 1:
            for copy in col_copies[4:]:
                copy.wait()
        if n < 3:
            fill(n + 1)
        tile = jnp.dot(left[...], right[n % 2][...], preferred_element_type=jnp.float32)
        if n == 0:
            for copy in got_copies:
                copy.wait()
        h = n % 2
        side = place[3] + n//2 - 2*place[3]*(n//2)
        at = pl.multiple_of(side*256, 256)
        for o in range(2):
            one = tile[0:256, o*256:(o+1)*256]
            two = tile[256:512, o*256:(o+1)*256]
            if got:
                more = come[h, o, :, pl.ds(at, 256)].astype(jnp.float32)
                one, two = (one + more, two) if h == 0 else (one, two + more)
            ready[n, 0, o] = one.astype(jnp.bfloat16)
            ready[n, 1, o] = two.astype(jnp.bfloat16)
        wide = pl.ds(pl.multiple_of(h*512 + at, 256), 256)
        if got:
            first = outs[0].at[:, :, wide]
        else:
            first = outs[h].at[:, :, pl.ds(at, 256)]
        for b, to in enumerate((first, outs[-1].at[:, :, wide])):
            copy = pltpu.make_async_copy(ready.at[n, b], to, out_sem.at[n, b])
            copy.start()
            leaving.append(copy)
    for copy in leaving:
        copy.wait()


def product(place, rows, own, other, got):
    wide = jax.ShapeDtypeStruct((2, 256, 1024), jnp.bfloat16)
    slim = jax.ShapeDtypeStruct((2, 256, 512), jnp.bfloat16)
    shapes = [wide, wide] if got else [slim, slim, wide]
    anywhere = pl.BlockSpec(memory_space=pl.ANY)
    return pl.pallas_call(
        product_kernel,
        grid_spec=pltpu.PrefetchScalarGridSpec(
            num_scalar_prefetch=1, grid=(1,),
            in_specs=[anywhere]*(12 + len(got)),
            out_specs=[anywhere]*len(shapes),
            scratch_shapes=[
                pltpu.VMEM((512, 2048), jnp.bfloat16),
                pltpu.VMEM((8, 4, 128, 512), jnp.bfloat16),
                pltpu.VMEM((2, 2, 256, 512), jnp.bfloat16),
                pltpu.VMEM((4, 2, 2, 256, 256), jnp.bfloat16),
                pltpu.VMEM((2048, 512), jnp.bfloat16),
                pltpu.VMEM((2048, 512), jnp.bfloat16),
                pltpu.SemaphoreType.DMA((4, 4)),
                pltpu.SemaphoreType.DMA((8,)),
                pltpu.SemaphoreType.DMA((2,)),
                pltpu.SemaphoreType.DMA((4, 2)),
            ],
        ),
        out_shape=shapes,
        compiler_params=pltpu.CompilerParams(vmem_limit_bytes=30*2**20),
        cost_estimate=pl.CostEstimate(flops=2**10, bytes_accessed=2**10, transcendentals=0),
        name="product",
    )(place, *rows, *own, *other, *got)


def total_kernel(a, b, c, *rest):
    out = rest[-1]
    t = a[...].astype(jnp.float32) + b[...].astype(jnp.float32) + c[...].astype(jnp.float32)
    out[:, 0, :] = t[0]
    out[:, 1, :] = t[1]


def total(parts, chunk, before):
    spec = pl.BlockSpec((2, 128, 1024), lambda n: (0, n, 0))
    more = [] if before is None else [before]
    return pl.pallas_call(
        total_kernel,
        grid=(2,),
        in_specs=[spec]*3 + [pl.BlockSpec(memory_space=pl.ANY)]*len(more),
        out_specs=pl.BlockSpec((128, 2, 1024), lambda n: (n, 0, chunk)),
        out_shape=jax.ShapeDtypeStruct((256, 2, 2048), jnp.float32),
        input_output_aliases={3: 0} if more else {},
        compiler_params=pltpu.CompilerParams(vmem_limit_bytes=30*2**20),
        cost_estimate=pl.CostEstimate(flops=2**10, bytes_accessed=2**10, transcendentals=0),
        name="total",
    )(*parts, *more)


def ring(shift):
    return [(i, (i + shift) % 4) for i in range(4)]


def along_z(block, shift):
    place = lambda z: (z % 2)*2 + z//2
    return lax.ppermute(block, ("zl", "zh"), [(place(i), place((i + shift) % 4)) for i in range(4)])


def after(arrays, *first):
    return lax.optimization_barrier((tuple(arrays), first))[0]


def swapped(blocks):
    return [lax.ppermute(a, "core", [(0, 1), (1, 0)]) for a in blocks]


def local(valence_index, conduction_index, valence_waves, conduction_waves,
          valence_energy, conduction_energy, frequency, sphere_map):
    x, y = lax.axis_index("x"), lax.axis_index("y")
    zl, zh, core = lax.axis_index("zl"), lax.axis_index("zh"), lax.axis_index("core")
    vb, cb = (y*2 + zl)*8, (x*2 + zh)*8
    val = lax.dynamic_slice(valence_waves, (vb, 0, 0), (8, 2, 32768)).reshape(8, 2, 256, 128)
    con = lax.dynamic_slice(conduction_waves, (cb, 0, 0), (8, 2, 32768)).reshape(8, 2, 256, 128)
    channel = lax.iota(jnp.int32, 128)[:, None] % 64
    band = lax.iota(jnp.int32, 64)[None, :]
    gap = jnp.sum(
        jnp.where(band == cb + channel % 8, conduction_energy[None, :], 0.0)
        - jnp.where(band == vb + channel//8, valence_energy[None, :], 0.0), axis=1)
    weight = 4.0 * gap / (gap*gap + frequency[0]*frequency[0]) / 4096
    scale = jnp.sqrt(weight / 32768.0)[None, :]
    ky = (sphere_map >> 5) & 31
    pos = ((ky & 7)*32 + (sphere_map >> 10))*128 + (ky >> 3)*32 + (sphere_map & 31)
    where = jnp.stack([x, y, zh*2 + zl, core]).astype(jnp.int32)
    parts = densities(pos, where, val, con, scale)
    row = [parts[0]] + [None]*3
    col = [parts[4]] + [None]*3
    for s in (2, 1, 3):
        row[s] = lax.ppermute(parts[s], "x", ring(s))
        col[s] = lax.ppermute(parts[4 + s], "y", ring(s))
    row_a, col_a = jnp.stack([r[:512] for r in row]), jnp.stack([c[:, :512] for c in col])
    row_b, col_b = jnp.stack([r[512:] for r in row]), jnp.stack([c[:, 512:] for c in col])
    rows_a, own_a = [row_a] + [None]*3, [col_a] + [None]*3
    for s in (1, 3):
        rows_a[s] = lax.ppermute(row_a, "y", ring(s))
        own_a[s] = lax.ppermute(col_a, "x", ring(s))
    rows_a[2] = lax.ppermute(row_a, "y", ring(2))
    col_a = after((col_a,), own_a[1], own_a[3])[0]
    own_a[2] = lax.ppermute(col_a, "x", ring(2))
    other_a = swapped(own_a)
    row_b, col_b = after((row_b, col_b), rows_a[2], own_a[2], other_a[0], other_a[1], other_a[3])
    rows_b, own_b = [row_b] + [None]*3, [col_b] + [None]*3
    for s in (1, 3):
        rows_b[s] = lax.ppermute(row_b, "y", ring(s))
        own_b[s] = lax.ppermute(col_b, "x", ring(s))
    own_b[2] = lax.ppermute(col_b, "x", ring(2))
    far0, far1, mine_a = product(where, rows_a, own_a, other_a, [])
    got_a = [along_z(far0, 1), along_z(far1, -1)]
    rows_b[2] = lax.ppermute(after((row_b,), far0, rows_b[1], rows_b[3])[0], "y", ring(2))
    other_b = swapped(after(own_b, far0))
    far0, far1, mine_b = product(where, rows_a, own_b, other_b, [])
    got_b = [along_z(far0, 1), along_z(far1, -1)]
    up_a, down_a = product(where, rows_b, own_a, other_a, got_a)
    done_a = [mine_a, along_z(up_a, 1), along_z(down_a, -1)]
    up_b, down_b = product(where, rows_b, own_b, other_b, got_b)
    done_b = [mine_b, along_z(up_b, 1), along_z(down_b, -1)]
    return total(done_b, 1, total(done_a, 0, None))


def solution(mesh):
    shaped = Mesh(mesh.devices.reshape(4, 2, 2, 2, 4), ("x", "zl", "zh", "core", "y"))
    split = P(("x", "zl", "zh", "core", "y"))
    return jax.shard_map(
        local,
        mesh=shaped,
        in_specs=(split, split, P(), P(), P(), P(), P(), P()),
        out_specs=P(("x", "zl", "zh", "core"), None, "y"),
        check_vma=False,
    )
```

```python
import numpy as np
import jax, jax.numpy as jnp
from jax import lax
from jax.experimental import pallas as pl
from jax.sharding import Mesh, PartitionSpec as P
from jax.experimental.pallas import tpu as pltpu

VMEM = 63*2**20


def tables():
    x = np.arange(32); e = np.arange(8); b = np.arange(4)
    ka, kx = np.meshgrid(e, x, indexing="ij")
    xx, yh = np.meshgrid(x, e, indexing="ij")
    ph = (kx.reshape(-1,1)*xx.reshape(1,-1) + 4*ka.reshape(-1,1)*yh.reshape(1,-1)) % 32
    c, s = np.cos(2*np.pi*ph/32), np.sin(2*np.pi*ph/32)
    first = np.block([[c, s], [-s, c]])
    second = []
    kb, kz = np.meshgrid(b, x, indexing="ij")
    yl, z = np.meshgrid(b, x, indexing="ij")
    for a in range(8):
        ky = a + 8*kb.reshape(-1,1)
        ph = (kz.reshape(-1,1)*z.reshape(1,-1) + ky*yl.reshape(1,-1)) % 32
        second.append(np.concatenate([np.cos(2*np.pi*ph/32), np.sin(2*np.pi*ph/32)], 1))
    return first.astype(jnp.bfloat16), np.stack(second).astype(jnp.bfloat16)

def density_kernel(pos, place, val, con, first, second, scale, *rest):
    outs, (xs, yr, yi, zt, held, turned, row_sem, col_sem) = rest[:8], rest[8:]
    step = pl.program_id(0)
    for v in (2*step, 2*step + 1):
        vr = val[v, 0].astype(jnp.float32)
        vi = val[v, 1].astype(jnp.float32)
        for pair in range(4):
            for k in range(2):
                cr = con[2*pair+k, 0].astype(jnp.float32)
                ci = con[2*pair+k, 1].astype(jnp.float32)
                xs[0:256, k*128:(k+1)*128] = (vr*cr + vi*ci).astype(jnp.bfloat16)
                xs[256:512, k*128:(k+1)*128] = (vr*ci - vi*cr).astype(jnp.bfloat16)
            y = jnp.dot(first[...], xs[...], preferred_element_type=jnp.float32)
            for k in range(2):
                p = v*8 + 2*pair + k
                yr[pl.ds(p, 256, stride=72), :] = y[0:256, k*128:(k+1)*128]
                yi[pl.ds(p, 256, stride=72), :] = y[256:512, k*128:(k+1)*128]

    @pl.when(step == 3)
    def _():
        def side(r):
            ar = yr[pl.ds(pl.multiple_of(r*72, 8), 64), :].astype(jnp.bfloat16)
            ai = yi[pl.ds(pl.multiple_of(r*72, 8), 64), :].astype(jnp.bfloat16)
            return [jnp.concatenate([ar, ai], 1), jnp.concatenate([ai, -ar], 1)]
        @pl.loop(0, 128, unroll=32)
        def _(q):
            r = q*2
            right = jnp.concatenate(side(r) + side(r+1), 0)
            z = lax.dot_general(second[r // 32], right, (((1,), (1,)), ((), ())), preferred_element_type=jnp.float32)
            zt[pl.ds(pl.multiple_of(r*128, 128), 128), :] = z[:, 0:128]
            zt[pl.ds(pl.multiple_of(r*128+128, 128), 128), :] = z[:, 128:256]
        w = scale[...]
        @pl.loop(0, 16)
        def _(block):
            base = (block*2 + place[3])*256

            @pl.loop(0, 16, unroll=4)
            def _(q):
                rows = [zt[pl.ds(pos[base + q*16 + j], 1), :] for j in range(16)]
                t = jnp.concatenate(rows, 0) * w
                held[pl.ds(pl.multiple_of(block*256 + q*16, 16), 16), :] = t.astype(jnp.bfloat16)

        leaving = []
        for s in range(4):
            a = lax.rem(place[0]+s, 4)*1024
            for q, shift in enumerate((2, 0, 1, 3)):
                to = lax.rem(place[2]+shift, 4)
                block = lax.rem(to, 2)*2 + lax.div(to, 2)
                copy = pltpu.make_async_copy(
                    held.at[pl.ds(pl.multiple_of(a + block*256, 256), 256), :],
                    outs[s].at[q*256:(q+1)*256, :], row_sem.at[s, q])
                copy.start()
                leaving.append(copy)
        for s in range(4):
            b = lax.rem(place[1]+s, 4)*1024
            for q in range(4):
                turned[s, :, q*256:(q+1)*256] = held[pl.ds(pl.multiple_of(b + q*256, 256), 256), :].T
            copy = pltpu.make_async_copy(turned.at[s], outs[4+s], col_sem.at[s])
            copy.start()
            leaving.append(copy)
        for copy in leaving:
            copy.wait()


def densities(pos, place, val, con, scale):
    first, second = tables()
    full = lambda shape: pl.BlockSpec(shape, lambda i, *_: (0,)*len(shape))
    return pl.pallas_call(
        density_kernel,
        grid_spec=pltpu.PrefetchScalarGridSpec(
            num_scalar_prefetch=2, grid=(4,),
            in_specs=[full((8,2,256,128)), full((8,2,256,128)), full((512,512)), full((8,128,256)), full((1,128))],
            out_specs=[pl.BlockSpec(memory_space=pl.ANY)]*8,
            scratch_shapes=[pltpu.VMEM((512,256), jnp.bfloat16), pltpu.VMEM((256*72,128), jnp.float32),
                pltpu.VMEM((256*72,128), jnp.float32), pltpu.VMEM((32768,128), jnp.float32), pltpu.VMEM((4096,128), jnp.bfloat16),
                pltpu.VMEM((4,128,1024), jnp.bfloat16), pltpu.SemaphoreType.DMA((4,4)), pltpu.SemaphoreType.DMA((4,))],
        ),
        out_shape=[jax.ShapeDtypeStruct((1024,128), jnp.bfloat16)]*4 + [jax.ShapeDtypeStruct((128,1024), jnp.bfloat16)]*4,
        compiler_params=pltpu.CompilerParams(vmem_limit_bytes=50*2**20),
        name="densities",
    )(pos, place, val, con, jnp.asarray(first), jnp.asarray(second), scale)


def product_kernel(place, *refs):
    rows, cols, refs = refs[0:4], refs[4:12], refs[12:]
    got, refs = (refs[:2], refs[2:]) if len(refs) == 14 else ((), refs)
    outs = refs[:-10]
    left, panel, come, ready, right0, right1, row_sem, col_sem, got_sem, out_sem = refs[-10:]
    right = (right0, right1)
    row_copies = [
        pltpu.make_async_copy(
            rows[t].at[s], left.at[:, pl.ds((t*4 + s)*128, 128)], row_sem.at[t, s])
        for t in range(4) for s in range(4)]
    col_copies = [
        pltpu.make_async_copy(cols[q], panel.at[q], col_sem.at[q]) for q in range(8)]
    got_copies = [pltpu.make_async_copy(got[h], come.at[h], got_sem.at[h]) for h in range(len(got))]
    for copy in col_copies[:4] + row_copies + col_copies[4:] + got_copies:
        copy.start()

    def fill(n):
        into, h = right[n % 2], n % 2
        for t in range(4):
            for s in range(4):
                k = (t*4 + s)*128
                piece = panel[4*(n//2) + s, t, :, h*256:(h+1)*256]
                into[k:k+128, 0:256] = piece
                into[k:k+64, 256:512] = -piece[64:128]
                into[k+64:k+128, 256:512] = piece[0:64]

    for copy in col_copies[:4]:
        copy.wait()
    fill(0)
    for copy in row_copies:
        copy.wait()
    leaving = []
    for n in range(4):
        if n == 1:
            for copy in col_copies[4:]:
                copy.wait()
        if n < 3:
            fill(n + 1)
        tile = jnp.dot(left[...], right[n % 2][...], preferred_element_type=jnp.float32)
        if n == 0:
            for copy in got_copies:
                copy.wait()
        h = n % 2
        side = place[3] + n//2 - 2*place[3]*(n//2)
        at = pl.multiple_of(side*256, 256)
        for o in range(2):
            one = tile[0:256, o*256:(o+1)*256]
            two = tile[256:512, o*256:(o+1)*256]
            if got:
                more = come[h, o, :, pl.ds(at, 256)].astype(jnp.float32)
                one, two = (one + more, two) if h == 0 else (one, two + more)
            ready[n, 0, o] = one.astype(jnp.bfloat16)
            ready[n, 1, o] = two.astype(jnp.bfloat16)
        wide = pl.ds(pl.multiple_of(h*512 + at, 256), 256)
        if got:
            first = outs[0].at[:, :, wide]
        else:
            first = outs[h].at[:, :, pl.ds(at, 256)]
        for b, to in enumerate((first, outs[-1].at[:, :, wide])):
            copy = pltpu.make_async_copy(ready.at[n, b], to, out_sem.at[n, b])
            copy.start()
            leaving.append(copy)
    for copy in leaving:
        copy.wait()


def product(place, rows, own, other, got):
    wide = jax.ShapeDtypeStruct((2, 256, 1024), jnp.bfloat16)
    slim = jax.ShapeDtypeStruct((2, 256, 512), jnp.bfloat16)
    shapes = [wide, wide] if got else [slim, slim, wide]
    anywhere = pl.BlockSpec(memory_space=pl.ANY)
    return pl.pallas_call(
        product_kernel,
        grid_spec=pltpu.PrefetchScalarGridSpec(
            num_scalar_prefetch=1, grid=(1,),
            in_specs=[anywhere]*(12 + len(got)),
            out_specs=[anywhere]*len(shapes),
            scratch_shapes=[
                pltpu.VMEM((512, 2048), jnp.bfloat16),
                pltpu.VMEM((8, 4, 128, 512), jnp.bfloat16),
                pltpu.VMEM((2, 2, 256, 512), jnp.bfloat16),
                pltpu.VMEM((4, 2, 2, 256, 256), jnp.bfloat16),
                pltpu.VMEM((2048, 512), jnp.bfloat16),
                pltpu.VMEM((2048, 512), jnp.bfloat16),
                pltpu.SemaphoreType.DMA((4, 4)),
                pltpu.SemaphoreType.DMA((8,)),
                pltpu.SemaphoreType.DMA((2,)),
                pltpu.SemaphoreType.DMA((4, 2)),
            ],
        ),
        out_shape=shapes,
        compiler_params=pltpu.CompilerParams(vmem_limit_bytes=20*2**20),
        cost_estimate=pl.CostEstimate(flops=2**10, bytes_accessed=2**10, transcendentals=0),
        name="product",
    )(place, *rows, *own, *other, *got)


def total_kernel(a, b, c, *rest):
    out = rest[-1]
    t = a[...].astype(jnp.float32) + b[...].astype(jnp.float32) + c[...].astype(jnp.float32)
    out[:, 0, :] = t[0]
    out[:, 1, :] = t[1]


def total(parts, chunk, before):
    spec = pl.BlockSpec((2, 128, 1024), lambda n: (0, n, 0))
    more = [] if before is None else [before]
    return pl.pallas_call(
        total_kernel,
        grid=(2,),
        in_specs=[spec]*3 + [pl.BlockSpec(memory_space=pl.ANY)]*len(more),
        out_specs=pl.BlockSpec((128, 2, 1024), lambda n: (n, 0, chunk)),
        out_shape=jax.ShapeDtypeStruct((256, 2, 2048), jnp.float32),
        input_output_aliases={3: 0} if more else {},
        compiler_params=pltpu.CompilerParams(vmem_limit_bytes=20*2**20),
        cost_estimate=pl.CostEstimate(flops=2**10, bytes_accessed=2**10, transcendentals=0),
        name="total",
    )(*parts, *more)


def ring(shift):
    return [(i, (i + shift) % 4) for i in range(4)]


def along_z(block, shift):
    place = lambda z: (z % 2)*2 + z//2
    return lax.ppermute(block, ("zl", "zh"), [(place(i), place((i + shift) % 4)) for i in range(4)])


def after(arrays, *first):
    return lax.optimization_barrier((tuple(arrays), first))[0]


def swapped(blocks):
    return [lax.ppermute(a, "core", [(0, 1), (1, 0)]) for a in blocks]


def local(valence_index, conduction_index, valence_waves, conduction_waves,
          valence_energy, conduction_energy, frequency, sphere_map):
    x, y = lax.axis_index("x"), lax.axis_index("y")
    zl, zh, core = lax.axis_index("zl"), lax.axis_index("zh"), lax.axis_index("core")
    vb, cb = (y*2 + zl)*8, (x*2 + zh)*8
    val = lax.dynamic_slice(valence_waves, (vb, 0, 0), (8, 2, 32768)).reshape(8, 2, 256, 128)
    con = lax.dynamic_slice(conduction_waves, (cb, 0, 0), (8, 2, 32768)).reshape(8, 2, 256, 128)
    channel = lax.iota(jnp.int32, 128)[:, None] % 64
    band = lax.iota(jnp.int32, 64)[None, :]
    gap = jnp.sum(
        jnp.where(band == cb + channel % 8, conduction_energy[None, :], 0.0)
        - jnp.where(band == vb + channel//8, valence_energy[None, :], 0.0), axis=1)
    weight = 4.0 * gap / (gap*gap + frequency[0]*frequency[0]) / 4096
    scale = jnp.sqrt(weight / 32768.0)[None, :]
    ky = (sphere_map >> 5) & 31
    pos = ((ky & 7)*32 + (sphere_map >> 10))*128 + (ky >> 3)*32 + (sphere_map & 31)
    where = jnp.stack([x, y, zh*2 + zl, core]).astype(jnp.int32)
    parts = densities(pos, where, val, con, scale)
    row = [parts[0]] + [None]*3
    col = [parts[4]] + [None]*3
    for s in (2, 1, 3):
        row[s] = lax.ppermute(parts[s], "x", ring(s))
        col[s] = lax.ppermute(parts[4 + s], "y", ring(s))
    row_a, col_a = jnp.stack([r[:512] for r in row]), jnp.stack([c[:, :512] for c in col])
    row_b, col_b = jnp.stack([r[512:] for r in row]), jnp.stack([c[:, 512:] for c in col])
    rows_a, own_a = [row_a] + [None]*3, [col_a] + [None]*3
    for s in (1, 3):
        rows_a[s] = lax.ppermute(row_a, "y", ring(s))
        own_a[s] = lax.ppermute(col_a, "x", ring(s))
    rows_a[2] = lax.ppermute(row_a, "y", ring(2))
    col_a = after((col_a,), own_a[1], own_a[3])[0]
    own_a[2] = lax.ppermute(col_a, "x", ring(2))
    other_a = swapped(own_a)
    row_b, col_b = after((row_b, col_b), rows_a[2], own_a[2], other_a[0], other_a[1], other_a[3])
    rows_b, own_b = [row_b] + [None]*3, [col_b] + [None]*3
    for s in (1, 3):
        rows_b[s] = lax.ppermute(row_b, "y", ring(s))
        own_b[s] = lax.ppermute(col_b, "x", ring(s))
    own_b[2] = lax.ppermute(col_b, "x", ring(2))
    far0, far1, mine_a = product(where, rows_a, own_a, other_a, [])
    got_a = [along_z(far0, 1), along_z(far1, -1)]
    rows_b[2] = lax.ppermute(after((row_b,), far0, rows_b[1], rows_b[3])[0], "y", ring(2))
    other_b = swapped(after(own_b, far0))
    far0, far1, mine_b = product(where, rows_a, own_b, other_b, [])
    got_b = [along_z(far0, 1), along_z(far1, -1)]
    up_a, down_a = product(where, rows_b, own_a, other_a, got_a)
    done_a = [mine_a, along_z(up_a, 1), along_z(down_a, -1)]
    up_b, down_b = product(where, rows_b, own_b, other_b, got_b)
    done_b = [mine_b, along_z(up_b, 1), along_z(down_b, -1)]
    return total(done_b, 1, total(done_a, 0, None))


def solution(mesh):
    shaped = Mesh(mesh.devices.reshape(4, 2, 2, 2, 4), ("x", "zl", "zh", "core", "y"))
    split = P(("x", "zl", "zh", "core", "y"))
    return jax.shard_map(
        local,
        mesh=shaped,
        in_specs=(split, split, P(), P(), P(), P(), P(), P()),
        out_specs=P(("x", "zl", "zh", "core"), None, "y"),
        check_vma=False,
    )
```
